256 devices in a mesh: rows: 32 (over x, z_lo, core), ch: 8 (over y, z_hi).
Axes of the slice: x: 4, y: 4, z: 8 (z_hi: 2, z_lo: 4; z = z_hi * 4 + z_lo), core: 2. Of those that a mesh axis runs over, the one named last changes fastest.
Arguments:
- features: bfloat16 [1536, 32768], P('ch', 'rows'), may hold values from -6 to 6
- cotangent: bfloat16 [1536, 32768], P('ch', 'rows'), may hold values from -6 to 6
- blocks: bfloat16 [256, 128, 128], P('rows'), may hold values from -0.5 to 0.5
- twiddles: float32 [2, 8, 32768], P(None, None, 'rows'), may hold values from -0.75 to 0.85, as said below
- channel_weight: bfloat16 [1536, 1536], P('ch'), may hold values from -0.15625 to 0.15625
Outputs:
- grad_features: bfloat16 [1536, 32768], P('ch', 'rows')
- grad_weight: float32 [1536, 1536], P('ch', 'rows')
The draws below stay inside these ranges and needn't reach their ends.
Inputs may be any that keep to these rules, and one draw needn't show every extreme that they name: twiddles[0] lies in 0.55 to 0.85; twiddles[1] has magnitude 0.35 to 0.75 with either sign.
All inputs are finite; a program needn't handle non-finite values.
Results may differ from the reference program's by a relative error of at most 0.04.
Values may be sent and summed in bfloat16 or wider, within the bound.
A program may use at most 64 MiB of HBM per device.

```python
import jax
import jax.numpy as jnp
from jax import lax

C = 1536
BLOCK = 128
TOKENS = 32768
LEVELS = 8


def draw_twiddles(key, part):
    key = jax.random.fold_in(key, 7)
    first, second, third = jax.random.split(key, 3)
    shape = (LEVELS, TOKENS)
    own = jax.random.uniform(first, shape, jnp.float32, 0.6, 0.8)
    magnitude = jax.random.uniform(second, shape, jnp.float32, 0.4, 0.7)
    signs = jnp.where(jax.random.bernoulli(third, 0.5, shape), 1.0, -1.0).astype(jnp.float32)
    return jnp.stack([own, magnitude * signs]).astype(jnp.float32)


def raised(entries, stream_key, source, target, shards_of, factor):
    def block_of(position):
        return (jnp.arange(entries.shape[position]) // (entries.shape[position] // shards_of)).reshape((-1,) + (1,) * (entries.ndim - 1 - position))

    first = jax.random.permutation(stream_key, shards_of)[block_of(target)]
    other_side = (block_of(target) + shards_of // 2) % shards_of
    return jnp.where((block_of(source) == first) | (block_of(source) == other_side), factor * entries, entries)


def block_scale(key, extent, cuts, least, high):
    def one(axis_at, parts):
        draws = jax.random.uniform(jax.random.fold_in(jax.random.fold_in(key, 6), axis_at), (parts,), jnp.float32, least / len(cuts), high / len(cuts))
        return jnp.repeat(jnp.exp(draws), extent[axis_at] // parts).reshape((-1,) + (1,) * (len(extent) - axis_at - 1))

    loudness = one(*cuts[0])
    for cut in cuts[1:]:
        loudness = loudness * one(*cut)
    return loudness


def bell_draw(key, extent, spread, most, pieces=(), dtype=jnp.bfloat16):
    result = spread * jax.random.normal(key, extent, jnp.float32)
    if pieces:
        result = result * block_scale(key, extent, pieces, -0.22, 0.18)
    return jnp.clip(result, -most, most).astype(dtype)


def gaussian_with(stream_key, shape, scale, most, cuts, heavy, kind=jnp.bfloat16):
    drawn = scale * jax.random.normal(stream_key, shape, jnp.float32)
    if cuts:
        drawn = drawn * block_scale(stream_key, shape, cuts, -0.22, 0.18)
    return jnp.clip(raised(drawn, jax.random.fold_in(stream_key, 3), *heavy), -most, most).astype(kind)


def setup_inputs(seed: int = 0) -> dict:
    key_of = jax.random.split(jax.random.key(seed), 6)
    features = bell_draw(key_of[0], (C, TOKENS), 1.0, 6.0, ((0, 8), (1, 32)))
    cotangent = gaussian_with(key_of[1], (C, TOKENS), 1.0, 6.0, ((0, 8), (1, 32)), (1, 0, 32, 2.75))
    blocks = bell_draw(key_of[2], (TOKENS // BLOCK, BLOCK, BLOCK), BLOCK ** -0.5, 0.5, ((0, 32),))
    twiddles = draw_twiddles(jax.random.fold_in(key_of[5], 71), 0)
    channel_weight = bell_draw(key_of[4], (C, C), C ** -0.5, 0.15625, ((0, 8),))
    return dict(features=features, cotangent=cotangent, blocks=blocks, twiddles=twiddles, channel_weight=channel_weight)


def flip_pairs(h, dist):
    n = h.shape[1]
    r = h.reshape((h.shape[0], n // (2 * dist), 2, dist))
    return jnp.flip(r, 2).reshape(h.shape)


def gelu_value(v):
    return 0.5 * v * (1.0 + lax.erf(v * 0.7071067811865476))


def gelu_slope(v):
    return 0.5 * (1.0 + lax.erf(v * 0.7071067811865476)) + v * jnp.exp(-0.5 * v * v) * 0.3989422804014327


def reference(features, cotangent, blocks, twiddles, channel_weight):
    count = TOKENS // BLOCK
    grouped = features.reshape(C, count, BLOCK).transpose(1, 0, 2)

    def block_fwd(pair):
        return jnp.dot(pair[1], pair[0].T, preferred_element_type=jnp.float32).astype(jnp.bfloat16)

    mixed = lax.map(block_fwd, (blocks, grouped)).transpose(1, 0, 2).reshape(C, TOKENS)
    for level in range(LEVELS):
        dist = BLOCK * 2 ** level
        own = twiddles[0, level][None, :]
        other = twiddles[1, level][None, :]
        mixed = (own * mixed.astype(jnp.float32) + other * flip_pairs(mixed, dist).astype(jnp.float32)).astype(jnp.bfloat16)
    mixed_wide = mixed.astype(jnp.float32)
    activated = gelu_value(mixed_wide).astype(jnp.bfloat16)
    grad_weight = jnp.dot(activated, cotangent.T, preferred_element_type=jnp.float32) * (1.0 / (TOKENS ** 0.5))
    back = (jnp.dot(channel_weight, cotangent, preferred_element_type=jnp.float32) * gelu_slope(mixed_wide)).astype(jnp.bfloat16)
    for level in reversed(range(LEVELS)):
        dist = BLOCK * 2 ** level
        own = twiddles[0, level][None, :]
        other = twiddles[1, level][None, :]
        sent = (other * back.astype(jnp.float32)).astype(jnp.bfloat16)
        back = (own * back.astype(jnp.float32) + flip_pairs(sent, dist).astype(jnp.float32)).astype(jnp.bfloat16)

    def block_bwd(pair):
        return jnp.dot(pair[1], pair[0], preferred_element_type=jnp.float32).astype(jnp.bfloat16)

    back_groups = back.reshape(C, count, BLOCK).transpose(1, 0, 2)
    grad_features = lax.map(block_bwd, (blocks, back_groups)).transpose(1, 0, 2).reshape(C, TOKENS)
    return grad_features, grad_weight
```

```python
import jax
import jax.numpy as jnp
from jax import lax
from jax.experimental import pallas as pl
from jax.experimental.pallas import tpu as pltpu
from jax.sharding import PartitionSpec as P

MESH = pl.DeviceIdType.MESH
F32 = jnp.float32
BF16 = jnp.bfloat16

NX, NZ, NC, NY = 4, 4, 2, 4
ROWS = NX * NZ * NC
CHS = 2 * NY
BLK = 128
LOCAL = 3
LEVELS = 8
CHUNKS = 4


def gelu_parts(v):
    half = 0.5 * (1.0 + lax.erf(v * 0.7071067811865476))
    act = v * half
    slope = half + v * jnp.exp(-0.5 * v * v) * 0.3989422804014327
    return act, slope


def flip(v, dist):
    n = v.shape[0]
    h = v.reshape((n // (2 * dist), 2, dist) + v.shape[1:])
    h = jnp.concatenate([h[:, 1:], h[:, :1]], axis=1)
    return h.reshape(v.shape)


def body(
    feat_hbm, cot_hbm, blocks_hbm, tw_hbm, w_hbm,
    gf_ref, gw_ref,
    feat, blocks, tw, w, cot,
    twst, twz, twall, twb, twl, m0, gacc, act,
    s1, r1, s2, r2, s3, r3, s4, r4,
    gst, rc, p1, rx, p2, rz, fin,
    loc_sem, a2a_send, a2a_recv, tw_send, tw_recv,
    cz_send, cz_recv, cy_send, cy_recv, g_send, g_recv,
):
    row = lax.axis_index("rows")
    col = lax.axis_index("ch")
    x, zl, c = row // (NZ * NC), (row // NC) % NZ, row % NC
    y = col // 2
    zc = row % (NZ * NC)
    up = {"ch": ((y + 1) % NY) * 2 + col % 2}
    down = {"ch": ((y + NY - 1) % NY) * 2 + col % 2}
    across = {"ch": y * 2 + (1 - col % 2)}
    tok = feat.shape[1]
    chan = feat.shape[0]
    quarter = chan // NX

    loads = [
        pltpu.make_async_copy(feat_hbm, feat, loc_sem.at[0]),
        pltpu.make_async_copy(blocks_hbm, blocks, loc_sem.at[1]),
        pltpu.make_async_copy(tw_hbm, tw, loc_sem.at[2]),
        pltpu.make_async_copy(cot_hbm, cot.at[col], loc_sem.at[3]),
        pltpu.make_async_copy(w_hbm, w, loc_sem.at[4]),
    ]
    for load in loads:
        load.start()

    bar = pltpu.get_barrier_semaphore()

    def greet(i, carry):
        pl.semaphore_signal(bar, inc=1, device_id={"rows": (row + i) % ROWS}, device_id_type=MESH)
        return carry

    lax.fori_loop(1, ROWS, greet, 0)
    for peer in (up, down, across):
        pl.semaphore_signal(bar, inc=1, device_id=peer, device_id_type=MESH)

    loads[2].wait()
    for b in range(NZ * NC):
        part = tw[:, :, b * BLK : (b + 1) * BLK]
        twst[b] = part.reshape(2 * LEVELS, BLK).astype(BF16)
        for j in range(LOCAL):
            for s in range(2):
                twl[s, j, b] = jnp.broadcast_to(tw[s, j : j + 1, b * BLK : (b + 1) * BLK], (8, BLK))

    pl.semaphore_wait(bar, ROWS - 1 + 3)

    def twz_send(i, carry):
        other = (zc + i) % (NZ * NC)
        pltpu.make_async_remote_copy(
            src_ref=twst.at[other], dst_ref=twz.at[zc],
            send_sem=tw_send.at[0], recv_sem=tw_recv.at[0],
            device_id={"rows": x * (NZ * NC) + other}, device_id_type=MESH,
        ).start()
        return carry

    lax.fori_loop(1, NZ * NC, twz_send, 0)
    pltpu.make_async_copy(twst.at[zc], twz.at[zc], tw_recv.at[0]).start()

    loads[0].wait()
    loads[1].wait()
    for g in range(NZ * NC):
        m0[g] = lax.dot_general(
            feat[:, g * BLK : (g + 1) * BLK], blocks[g], (((1,), (1,)), ((), ())),
            preferred_element_type=F32,
        )

    def local_fwd(t, carry):
        rows8 = pl.ds(pl.multiple_of(t * 16, 16), 16)
        v = m0[:, rows8, :].reshape(NZ * NC, 2, 8, BLK)
        for j in range(LOCAL):
            v = v * twl[0, j][:, None] + flip(v, 2**j) * twl[1, j][:, None]
        v = v.reshape(NZ * NC, 16, BLK).astype(BF16)
        per = quarter // 16
        s1[t // per, :, pl.ds(pl.multiple_of((t % per) * 16, 16), 16), :] = v
        return carry

    lax.fori_loop(0, chan // 16, local_fwd, 0)

    def exchange(step, src, dst):
        def one(i, carry):
            other = (row + i) % ROWS
            pltpu.make_async_remote_copy(
                src_ref=src.at[other // 8, other % 8], dst_ref=dst.at[row // 8, row % 8],
                send_sem=a2a_send.at[step], recv_sem=a2a_recv.at[step],
                device_id={"rows": other}, device_id_type=MESH,
            ).start()
            return carry

        lax.fori_loop(1, ROWS, one, 0)
        pltpu.make_async_copy(
            src.at[row // 8, row % 8], dst.at[row // 8, row % 8], a2a_recv.at[step]
        ).start()

    def arrived(step, dst):
        pltpu.make_async_copy(dst, dst, a2a_recv.at[step]).wait()

    exchange(0, s1, r1)

    size = chan // CHUNKS

    def cz(k):
        part = pl.ds(k * size, size)
        return pltpu.make_async_remote_copy(
            src_ref=cot.at[col, part], dst_ref=cot.at[col, part],
            send_sem=cz_send.at[k], recv_sem=cz_recv.at[k],
            device_id=across, device_id_type=MESH,
        )

    def cy(way, owner, k, which):
        part = pl.ds(k * size, size)
        return pltpu.make_async_remote_copy(
            src_ref=cot.at[owner, part], dst_ref=cot.at[owner, part],
            send_sem=cy_send.at[which, k, way], recv_sem=cy_recv.at[which, k, way],
            device_id=(up, down)[way], device_id_type=MESH,
        )

    loads[3].wait()
    own_y = [cy(way, col, k, 0) for k in range(CHUNKS) for way in range(2)]
    own_z = [cz(k) for k in range(CHUNKS)]
    for copy in own_y:
        copy.start()
    for copy in own_z:
        copy.start()

    pltpu.make_async_copy(twz, twz, tw_recv.at[0]).wait()

    def twx_send(i, carry):
        other = (x + i) % NX
        pltpu.make_async_remote_copy(
            src_ref=twz, dst_ref=twall.at[x],
            send_sem=tw_send.at[1], recv_sem=tw_recv.at[1],
            device_id={"rows": other * (NZ * NC) + zc}, device_id_type=MESH,
        ).start()
        return carry

    lax.fori_loop(1, NX, twx_send, 0)
    pltpu.make_async_copy(twz, twall.at[x], tw_recv.at[1]).start()
    pltpu.make_async_copy(twall, twall, tw_recv.at[1]).wait()

    def spread(r, carry):
        t = twall[r // 8, r % 8].astype(F32)
        for j in range(LEVELS - LOCAL):
            for s in range(2):
                at = s * LEVELS + LOCAL + j
                twb[s, j, r] = jnp.broadcast_to(t[at : at + 1, :], (8, BLK))
        return carry

    lax.fori_loop(0, ROWS, spread, 0)

    def relay(which, base):
        sent = []
        for k in range(CHUNKS):
            way = 0 if k < CHUNKS // 2 else 1
            owner = ((y + NY - 1) % NY if way == 0 else (y + 1) % NY) * 2 + base
            cy(way, owner, k, which).wait_recv()
            copy = cy(way, owner, k, which + 1)
            copy.start()
            sent.append(copy)
        return sent

    relays = relay(0, col % 2)

    arrived(0, r1)

    def cross_fwd(t, carry):
        part = pl.ds(pl.multiple_of(t * 16, 16), 16)
        v = r1[:, :, part, :].astype(F32).reshape(ROWS, 2, 8, BLK)
        for j in range(LEVELS - LOCAL):
            v = v * twb[0, j][:, None] + flip(v, 2**j) * twb[1, j][:, None]
        s2[:, :, part, :] = v.reshape(NX, NZ * NC, 16, BLK).astype(BF16)
        return carry

    lax.fori_loop(0, quarter // 16, cross_fwd, 0)
    exchange(1, s2, r2)

    far = col - col % 2 + (1 - col % 2)
    far_y = []
    for k in range(CHUNKS):
        own_z[k].wait_recv()
        for way in range(2):
            copy = cy(way, far, k, 2)
            copy.start()
            far_y.append(copy)
    relays += relay(2, 1 - col % 2)

    for which in (0, 2):
        for k in range(CHUNKS):
            way = 1 if k < CHUNKS // 2 else 0
            cy(way, col, k, which).wait_recv()
    for which in (1, 3):
        for k in range(CHUNKS):
            way = 0 if k < CHUNKS // 2 else 1
            cy(way, col, k, which).wait_recv()

    loads[4].wait()

    def project(n, carry):
        part = pl.ds(pl.multiple_of(n * 256, 256), 256)
        piece = cot[:, :, part].reshape(CHS * chan, 256)
        gacc[:, part] = jnp.dot(w[...], piece, preferred_element_type=F32)
        return carry

    lax.fori_loop(0, tok // 256, project, 0)

    arrived(1, r2)

    def middle(q, carry):
        part = pl.ds(pl.multiple_of(q * quarter, 16), quarter)
        for b in range(NZ * NC):
            lanes = slice(b * BLK, (b + 1) * BLK)
            a, s = gelu_parts(r2[q, b].astype(F32))
            act[part, lanes] = a.astype(BF16)
            s3[q, b] = (gacc[part, lanes] * s).astype(BF16)
        return carry

    lax.fori_loop(0, NX, middle, 0)
    exchange(2, s3, r3)

    def weight(h, carry):
        g = lax.dot_general(
            cot[h], act[...], (((1,), (1,)), ((), ())), preferred_element_type=F32
        ).astype(BF16)
        for i in range(4):
            gst[i % 2, h // 2, (h % 2) * 2 + i // 2] = g[i * 48 : (i + 1) * 48]
        return carry

    lax.fori_loop(0, CHS, weight, 0)
    g_core = pltpu.make_async_remote_copy(
        src_ref=gst.at[1 - c], dst_ref=rc, send_sem=g_send.at[0], recv_sem=g_recv.at[0],
        device_id={"rows": row + 1 - 2 * c}, device_id_type=MESH,
    )
    g_core.start()
    g_core.wait_recv()
    for i in range(NX):
        p1[i] = (gst[c, i].astype(F32) + rc[i].astype(F32)).astype(BF16)

    def gx(i, carry):
        other = (x + i) % NX
        pltpu.make_async_remote_copy(
            src_ref=p1.at[other], dst_ref=rx.at[x], send_sem=g_send.at[1], recv_sem=g_recv.at[1],
            device_id={"rows": other * (NZ * NC) + zc}, device_id_type=MESH,
        ).start()
        return carry

    lax.fori_loop(1, NX, gx, 0)
    pltpu.make_async_copy(p1.at[x], rx.at[x], g_recv.at[1]).start()

    arrived(2, r3)

    def cross_bwd(t, carry):
        part = pl.ds(pl.multiple_of(t * 16, 16), 16)
        v = r3[:, :, part, :].astype(F32).reshape(ROWS, 2, 8, BLK)
        for j in reversed(range(LEVELS - LOCAL)):
            v = v * twb[0, j][:, None] + flip(v * twb[1, j][:, None], 2**j)
        s4[:, :, part, :] = v.reshape(NX, NZ * NC, 16, BLK).astype(BF16)
        return carry

    lax.fori_loop(0, quarter // 16, cross_bwd, 0)
    exchange(3, s4, r4)

    pltpu.make_async_copy(rx, rx, g_recv.at[1]).wait()
    for i in range(NZ):
        total = rx[0, i].astype(F32)
        for j in range(1, NX):
            total = total + rx[j, i].astype(F32)
        p2[i] = total.astype(BF16)

    def gz(i, carry):
        other = (zl + i) % NZ
        pltpu.make_async_remote_copy(
            src_ref=p2.at[other], dst_ref=rz.at[zl], send_sem=g_send.at[2], recv_sem=g_recv.at[2],
            device_id={"rows": x * (NZ * NC) + other * NC + c}, device_id_type=MESH,
        ).start()
        return carry

    lax.fori_loop(1, NZ, gz, 0)
    pltpu.make_async_copy(p2.at[zl], rz.at[zl], g_recv.at[2]).start()

    arrived(3, r4)

    def local_bwd(t, carry):
        per = quarter // 16
        v = r4[t // per, :, pl.ds(pl.multiple_of((t % per) * 16, 16), 16), :]
        v = v.astype(F32).reshape(NZ * NC, 2, 8, BLK)
        for j in reversed(range(LOCAL)):
            v = v * twl[0, j][:, None] + flip(v * twl[1, j][:, None], 2**j)
        v = v.reshape(NZ * NC, 16, BLK).astype(BF16)
        rows8 = pl.ds(pl.multiple_of(t * 16, 16), 16)
        for g in range(NZ * NC):
            feat[rows8, g * BLK : (g + 1) * BLK] = v[g]
        return carry

    lax.fori_loop(0, chan // 16, local_bwd, 0)
    for g in range(NZ * NC):
        lanes = slice(g * BLK, (g + 1) * BLK)
        gf_ref[:, lanes] = jnp.dot(
            feat[:, lanes], blocks[g], preferred_element_type=F32
        ).astype(BF16)

    pltpu.make_async_copy(rz, rz, g_recv.at[2]).wait()
    total = rz[0].astype(F32)
    for j in range(1, NZ):
        total = total + rz[j].astype(F32)
    fin[...] = jnp.zeros_like(fin)
    fin[:48, :chan] = total * (1.0 / (tok * ROWS) ** 0.5)
    gw_ref[...] = jnp.transpose(fin[...])[:chan, :48]

    for step, src in enumerate((s1, s2, s3, s4)):
        for part in (src.at[0:3], src.at[3, 0:7]):
            pltpu.make_async_copy(part, part, a2a_send.at[step]).wait()
    pltpu.make_async_copy(twst.at[0:7], twst.at[0:7], tw_send.at[0]).wait()
    pltpu.make_async_copy(twall.at[0:3], twall.at[0:3], tw_send.at[1]).wait()
    for copy in own_y + own_z + far_y + relays:
        copy.wait_send()
    g_core.wait_send()
    pltpu.make_async_copy(p1.at[0:3], p1.at[0:3], g_send.at[1]).wait()
    pltpu.make_async_copy(p2.at[0:3], p2.at[0:3], g_send.at[2]).wait()


def per_device(features, cotangent, blocks, twiddles, channel_weight):
    chan, tok = features.shape
    quarter = chan // NX
    nb = NZ * NC
    wide = channel_weight.shape[1]
    piece = (NX, nb, quarter, BLK)
    vm = pltpu.VMEM
    dma = pltpu.SemaphoreType.DMA
    scratch = [
        vm((chan, tok), BF16), vm(blocks.shape, BF16), vm(twiddles.shape, F32),
        vm(channel_weight.shape, BF16), vm((CHS, chan, tok), BF16),
        vm((nb, 2 * LEVELS, BLK), BF16), vm((nb, 2 * LEVELS, BLK), BF16),
        vm((NX, nb, 2 * LEVELS, BLK), BF16),
        vm((2, LEVELS - LOCAL, ROWS, 8, BLK), F32), vm((2, LOCAL, nb, 8, BLK), F32),
        vm((nb, chan, BLK), F32), vm((chan, tok), F32), vm((chan, tok), BF16),
        *[vm(piece, BF16)] * 8,
        vm((2, NX, NZ, 48, chan), BF16), vm((NX, NZ, 48, chan), BF16),
        vm((NX, NZ, 48, chan), BF16), vm((NX, NZ, 48, chan), BF16),
        vm((NZ, 48, chan), BF16), vm((NZ, 48, chan), BF16), vm((128, 256), F32),
        dma((5,)), dma((4,)), dma((4,)), dma((2,)), dma((2,)),
        dma((CHUNKS,)), dma((CHUNKS,)), dma((4, CHUNKS, 2)), dma((4, CHUNKS, 2)),
        dma((3,)), dma((3,)),
    ]
    return pl.pallas_call(
        body,
        out_shape=(
            jax.ShapeDtypeStruct((chan, tok), BF16),
            jax.ShapeDtypeStruct((chan, wide // ROWS), F32),
        ),
        in_specs=[pl.BlockSpec(memory_space=pl.ANY)] * 5,
        out_specs=(pl.BlockSpec(memory_space=pltpu.VMEM),) * 2,
        scratch_shapes=scratch,
        name="mixer",
        compiler_params=pltpu.CompilerParams(
            collective_id=0, has_side_effects=True, vmem_limit_bytes=48 << 20
        ),
    )(features, cotangent, blocks, twiddles, channel_weight)


def solution(mesh):
    return jax.shard_map(
        per_device,
        mesh=mesh,
        in_specs=(
            P("ch", "rows"),
            P("ch", "rows"),
            P("rows", None, None),
            P(None, None, "rows"),
            P("ch", None),
        ),
        out_specs=(P("ch", "rows"), P("ch", "rows")),
        check_vma=False,
    )
```

```python
import jax
import jax.numpy as jnp
from jax import lax
from jax.experimental import pallas as pl
from jax.experimental.pallas import tpu as pltpu
from jax.sharding import PartitionSpec as P

MESH = pl.DeviceIdType.MESH
F32 = jnp.float32
BF16 = jnp.bfloat16

NX, NZ, NC, NY = 4, 4, 2, 4
ROWS = NX * NZ * NC
NB = NZ * NC
CHS = 2 * NY
BLK = 128
LOCAL = 3
LEVELS = 8
CROSS = LEVELS - LOCAL
CHUNKS = NZ
TILE = 16


def gelu_parts(v):
    half = 0.5 * (1.0 + lax.erf(v * 0.7071067811865476))
    act = v * half
    slope = half + v * jnp.exp(-0.5 * v * v) * 0.3989422804014327
    return act, slope


def flip(v, dist):
    n = v.shape[0]
    h = v.reshape((n // (2 * dist), 2, dist) + v.shape[1:])
    h = jnp.concatenate([h[:, 1:], h[:, :1]], axis=1)
    return h.reshape(v.shape)


def span(start, size):
    return pl.ds(pl.multiple_of(start, size), size)


def body(
    feat_hbm, cot_hbm, blocks_hbm, tw_hbm, w_hbm,
    gf_ref, gw_ref,
    feat, blocks, tw, w, cot,
    twst, twz, twall, twb, twl, m0, act, slope,
    s1, r1, s2, s3, r3, s4, r4, bk,
    gst, rc, p1, rx, p2, rz,
    loc_sem, snd0, snd1, snd2, snd3, rcv0, rcv1, rcv2, rcv3, tw_send, tw_recv,
    cz_send, cz_recv, cy_send, cy_recv, g_send, g_recv,
):
    a2a_send, a2a_recv = (snd0, snd1, snd2, snd3), (rcv0, rcv1, rcv2, rcv3)
    row = lax.axis_index("rows")
    col = lax.axis_index("ch")
    x, zl, c = row // NB, (row // NC) % NZ, row % NC
    y, zh = col // 2, col % 2
    zc = row % NB
    up = {"ch": ((y + 1) % NY) * 2 + zh}
    down = {"ch": ((y + NY - 1) % NY) * 2 + zh}
    across = {"ch": y * 2 + (1 - zh)}
    chan, tok = feat.shape
    quarter = chan // NX
    tiles = quarter // TILE
    size = tok // CHUNKS
    group = gw_ref.shape[0]

    loads = [
        pltpu.make_async_copy(cot_hbm, cot.at[col], loc_sem.at[0]),
        pltpu.make_async_copy(tw_hbm, tw, loc_sem.at[1]),
        pltpu.make_async_copy(feat_hbm, feat, loc_sem.at[2]),
        pltpu.make_async_copy(blocks_hbm, blocks, loc_sem.at[3]),
        pltpu.make_async_copy(w_hbm, w, loc_sem.at[4]),
    ]
    for load in loads:
        load.start()

    bar = pltpu.get_barrier_semaphore()

    def greet(i, carry):
        pl.semaphore_signal(bar, inc=1, device_id={"rows": (row + i) % ROWS}, device_id_type=MESH)
        return carry

    lax.fori_loop(1, ROWS, greet, 0)
    for peer in (up, down, across):
        pl.semaphore_signal(bar, inc=1, device_id=peer, device_id_type=MESH)

    def local_fwd(t):
        for g in range(NB):
            lanes = slice(g * BLK, (g + 1) * BLK)
            left = jnp.concatenate(
                [feat[span(q * quarter + t * TILE, TILE), lanes] for q in range(NX)], axis=0
            )
            m0[g] = lax.dot_general(
                left, blocks[g], (((1,), (1,)), ((), ())), preferred_element_type=F32
            )

        def local_one(q, carry):
            v = m0[:, span(q * TILE, TILE), :].reshape(NB, 2, 8, BLK)
            for j in range(LOCAL):
                v = v * twl[0, j][:, None] + flip(v, 2**j) * twl[1, j][:, None]
            s1[q, :, span(t * TILE, TILE), :] = v.reshape(NB, TILE, BLK).astype(BF16)
            return carry

        lax.fori_loop(0, NX, local_one, 0)

    loads[1].wait()
    for b in range(NB):
        lanes = slice(b * BLK, (b + 1) * BLK)
        twst[b] = tw[:, :, lanes].reshape(2 * LEVELS, BLK).astype(BF16)

    loads[0].wait()
    pl.semaphore_wait(bar, ROWS - 1 + 3)

    def twz_send(i, carry):
        other = (zc + i) % NB
        pltpu.make_async_remote_copy(
            src_ref=twst.at[other], dst_ref=twz.at[zc],
            send_sem=tw_send.at[0], recv_sem=tw_recv.at[0],
            device_id={"rows": x * NB + other}, device_id_type=MESH,
        ).start()
        return carry

    lax.fori_loop(1, NB, twz_send, 0)
    pltpu.make_async_copy(twst.at[zc], twz.at[zc], tw_recv.at[0]).start()

    def exchange(step, t, src, dst, sem):
        part = span(t * TILE, TILE)

        def exch_one(i, carry):
            other = (row + i) % ROWS
            pltpu.make_async_remote_copy(
                src_ref=src.at[other // NB, other % NB, part], dst_ref=dst(row, part),
                send_sem=a2a_send[step].at[0], recv_sem=sem,
                device_id={"rows": other}, device_id_type=MESH,
            ).start()
            return carry

        lax.fori_loop(1, ROWS, exch_one, 0)
        pltpu.make_async_copy(src.at[x, zc, part], dst(row, part), sem).start()

    def slots(ref):
        return lambda r, part: ref.at[r // NB, r % NB, part]

    def arrived(step, t, ref):
        ref = ref.at[:, :, span(t * TILE, TILE)]
        pltpu.make_async_copy(ref, ref, a2a_recv[step].at[t]).wait()

    def chunk(k):
        return span(((zl + 1 + k) % NZ) * size, size)

    def cz(k):
        return pltpu.make_async_remote_copy(
            src_ref=cot.at[col, :, chunk(k)], dst_ref=cot.at[col, :, chunk(k)],
            send_sem=cz_send.at[k], recv_sem=cz_recv.at[k],
            device_id=across, device_id_type=MESH,
        )

    def cy(which, k, way, owner):
        return pltpu.make_async_remote_copy(
            src_ref=cot.at[owner, :, chunk(k)], dst_ref=cot.at[owner, :, chunk(k)],
            send_sem=cy_send.at[which, k, way], recv_sem=cy_recv.at[which, k, way],
            device_id=(up, down)[way], device_id_type=MESH,
        )

    sent = []

    def go(copy):
        copy.start()
        sent.append(copy)

    for k in range(CHUNKS):
        go(cz(k))
        for way in range(2):
            go(cy(0, k, way, col))

    for b in range(NB):
        lanes = slice(b * BLK, (b + 1) * BLK)
        for j in range(LOCAL):
            for s in range(2):
                twl[s, j, b] = jnp.broadcast_to(tw[s, j : j + 1, lanes], (8, BLK))

    loads[2].wait()
    loads[3].wait()
    for t in range(tiles):
        local_fwd(t)

    def relay(which, k):
        way = k % 2
        owner = ((y + NY - 1) % NY if way == 0 else (y + 1) % NY) * 2
        owner = owner + (zh if which == 0 else 1 - zh)
        cy(which, k, way, owner).wait_recv()
        go(cy(which + 1, k, way, owner))

    def far_send(k):
        cz(k).wait_recv()
        for way in range(2):
            go(cy(2, k, way, y * 2 + (1 - zh)))

    def spread(r, carry):
        u = twall[r // NB, r % NB].astype(F32)
        for j in range(CROSS):
            for s in range(2):
                at = s * LEVELS + LOCAL + j
                twb[s, j, r] = jnp.broadcast_to(u[at : at + 1, :], (8, BLK))
        return carry


    def cross_fwd(t):
        part = span(t * TILE, TILE)
        arrived(0, t, r1)
        v = r1[:, :, part, :].astype(F32).reshape(ROWS, 2, 8, BLK)
        for j in range(CROSS):
            v = v * twb[0, j][:, None] + flip(v, 2**j) * twb[1, j][:, None]
        slope[:, :, part, :] = v.reshape(NX, NB, TILE, BLK)

        def gelu_one(r, carry):
            a, s = gelu_parts(slope[r // NB, r % NB, part, :])
            s2[r // NB, r % NB, part, :] = a.astype(BF16)
            slope[r // NB, r % NB, part, :] = s
            return carry

        lax.fori_loop(0, ROWS, gelu_one, 0)
        exchange(
            1, t, s2,
            lambda r, _: act.at[span((r // NB) * quarter + t * TILE, TILE), span((r % NB) * BLK, BLK)],
            a2a_recv[1].at[0],
        )

    def project(k):
        way = k % 2
        for which in range(4):
            cy(which, k, way if which % 2 else 1 - way, col).wait_recv()
        piece = cot[:, :, chunk(k)].reshape(CHS * chan, size)
        back = jnp.dot(w[...], piece, preferred_element_type=F32).astype(BF16)
        first = ((zl + 1 + k) % NZ) * NC
        for q in range(NX):
            for j in range(NC):
                s3[q, first + j] = back[q * quarter : (q + 1) * quarter, j * BLK : (j + 1) * BLK]
        last = k == CHUNKS - 1
        for t in range(tiles):
            part = slice(t * TILE, (t + 1) * TILE)

            def a3_one(i, carry):
                at = (x * NC + c + i) % NB
                q, b = at // NC, first + at % NC
                pltpu.make_async_remote_copy(
                    src_ref=s3.at[q, b, part], dst_ref=r3.at[x, zc, part],
                    send_sem=a2a_send[2].at[0], recv_sem=a2a_recv[2].at[t],
                    device_id={"rows": q * NB + b}, device_id_type=MESH,
                ).start()
                return carry

            lax.fori_loop(1 if last else 0, NB, a3_one, 0)
            if last:
                pltpu.make_async_copy(
                    s3.at[x, zc, part], r3.at[x, zc, part], a2a_recv[2].at[t]
                ).start()

    relay(0, 0)
    pltpu.make_async_copy(twz, twz, tw_recv.at[0]).wait()

    def twx_send(i, carry):
        other = (x + i) % NX
        pltpu.make_async_remote_copy(
            src_ref=twz, dst_ref=twall.at[x],
            send_sem=tw_send.at[1], recv_sem=tw_recv.at[1],
            device_id={"rows": other * NB + zc}, device_id_type=MESH,
        ).start()
        return carry

    lax.fori_loop(1, NX, twx_send, 0)
    pltpu.make_async_copy(twz, twall.at[x], tw_recv.at[1]).start()

    relay(0, 1)
    far_send(0)
    for t in range(tiles):
        exchange(0, t, s1, slots(r1), a2a_recv[0].at[t])
    relay(0, 2)
    pltpu.make_async_copy(twall, twall, tw_recv.at[1]).wait()
    lax.fori_loop(0, ROWS, spread, 0)
    far_send(1)
    relay(2, 0)
    relay(0, 3)
    far_send(2)
    relay(2, 1)
    cross_fwd(0)
    far_send(3)
    relay(2, 2)
    cross_fwd(1)
    loads[4].wait()
    relay(2, 3)
    cross_fwd(2)
    project(0)
    project(1)
    project(2)
    project(3)

    pltpu.make_async_copy(act, act, a2a_recv[1].at[0]).wait()

    def weight(h, carry):
        g = lax.dot_general(
            cot[h], act[...], (((1,), (1,)), ((), ())), preferred_element_type=F32
        ).astype(BF16)
        for i in range(4):
            gst[i % 2, h // 2, (h % 2) * 2 + i // 2] = g[i * group : (i + 1) * group]
        return carry

    lax.fori_loop(0, CHS, weight, 0)
    g_core = pltpu.make_async_remote_copy(
        src_ref=gst.at[1 - c], dst_ref=rc, send_sem=g_send.at[0], recv_sem=g_recv.at[0],
        device_id={"rows": row + 1 - 2 * c}, device_id_type=MESH,
    )
    go(g_core)

    def cross_bwd(t):
        part = span(t * TILE, TILE)
        arrived(2, t, r3)
        v = r3[:, :, part, :].astype(F32) * slope[:, :, part, :]
        v = v.reshape(ROWS, 2, 8, BLK)
        for j in reversed(range(CROSS)):
            v = v * twb[0, j][:, None] + flip(v * twb[1, j][:, None], 2**j)
        s4[:, :, part, :] = v.reshape(NX, NB, TILE, BLK).astype(BF16)
        exchange(3, t, s4, slots(r4), a2a_recv[3].at[t])

    for t in range(tiles):
        cross_bwd(t)

    g_core.wait_recv()
    for i in range(NX):
        p1[i] = (gst[c, i].astype(F32) + rc[i].astype(F32)).astype(BF16)

    def gx(i, carry):
        other = (x + i) % NX
        pltpu.make_async_remote_copy(
            src_ref=p1.at[other], dst_ref=rx.at[x], send_sem=g_send.at[1], recv_sem=g_recv.at[1],
            device_id={"rows": other * NB + zc}, device_id_type=MESH,
        ).start()
        return carry

    lax.fori_loop(1, NX, gx, 0)
    pltpu.make_async_copy(p1.at[x], rx.at[x], g_recv.at[1]).start()

    def local_bwd(t):
        arrived(3, t, r4)

        def bwd_one(q, carry):
            v = r4[q, :, span(t * TILE, TILE), :].astype(F32).reshape(NB, 2, 8, BLK)
            for j in reversed(range(LOCAL)):
                v = v * twl[0, j][:, None] + flip(v * twl[1, j][:, None], 2**j)
            bk[:, span(q * TILE, TILE), :] = v.reshape(NB, TILE, BLK).astype(BF16)
            return carry

        lax.fori_loop(0, NX, bwd_one, 0)
        for g in range(NB):
            out = jnp.dot(bk[g], blocks[g], preferred_element_type=F32).astype(BF16)
            for q in range(NX):
                gf_ref[span(q * quarter + t * TILE, TILE), g * BLK : (g + 1) * BLK] = out[
                    q * TILE : (q + 1) * TILE
                ]

    local_bwd(0)
    pltpu.make_async_copy(rx, rx, g_recv.at[1]).wait()
    for i in range(NZ):
        total = rx[0, i].astype(F32)
        for j in range(1, NX):
            total = total + rx[j, i].astype(F32)
        p2[i] = total.astype(BF16)

    def gz(i, carry):
        other = (zl + i) % NZ
        pltpu.make_async_remote_copy(
            src_ref=p2.at[other], dst_ref=rz.at[zl], send_sem=g_send.at[2], recv_sem=g_recv.at[2],
            device_id={"rows": x * NB + other * NC + c}, device_id_type=MESH,
        ).start()
        return carry

    lax.fori_loop(1, NZ, gz, 0)
    pltpu.make_async_copy(p2.at[zl], rz.at[zl], g_recv.at[2]).start()

    for t in range(1, tiles):
        local_bwd(t)

    pltpu.make_async_copy(rz, rz, g_recv.at[2]).wait()
    total = rz[0].astype(F32)
    for j in range(1, NZ):
        total = total + rz[j].astype(F32)
    gw_ref[...] = total * (1.0 / (tok * ROWS) ** 0.5)

    for step, src in enumerate((s1, s2, s3, s4)):
        for part in (src.at[0:3], src.at[3, 0:7]):
            pltpu.make_async_copy(part, part, a2a_send[step].at[0]).wait()
    pltpu.make_async_copy(twst.at[0:7], twst.at[0:7], tw_send.at[0]).wait()
    pltpu.make_async_copy(twall.at[0:3], twall.at[0:3], tw_send.at[1]).wait()
    for copy in sent:
        copy.wait_send()
    pltpu.make_async_copy(p1.at[0:3], p1.at[0:3], g_send.at[1]).wait()
    pltpu.make_async_copy(p2.at[0:3], p2.at[0:3], g_send.at[2]).wait()


def per_device(features, cotangent, blocks, twiddles, channel_weight):
    chan, tok = features.shape
    quarter = chan // NX
    group = channel_weight.shape[1] // ROWS
    piece = (NX, NB, quarter, BLK)
    vm = pltpu.VMEM
    dma = pltpu.SemaphoreType.DMA
    scratch = [
        vm((chan, tok), BF16), vm(blocks.shape, BF16), vm(twiddles.shape, F32),
        vm(channel_weight.shape, BF16), vm((CHS, chan, tok), BF16),
        vm((NB, 2 * LEVELS, BLK), BF16), vm((NB, 2 * LEVELS, BLK), BF16),
        vm((NX, NB, 2 * LEVELS, BLK), BF16),
        vm((2, CROSS, ROWS, 8, BLK), F32), vm((2, LOCAL, NB, 8, BLK), F32),
        vm((NB, NX * TILE, BLK), F32), vm((chan, tok), BF16), vm(piece, F32),
        *[vm(piece, BF16)] * 7, vm((NB, NX * TILE, BLK), BF16),
        vm((NC, NX, NZ, group, chan), BF16), vm((NX, NZ, group, chan), BF16),
        vm((NX, NZ, group, chan), BF16), vm((NX, NZ, group, chan), BF16),
        vm((NZ, group, chan), BF16), vm((NZ, group, chan), BF16),
        dma((5,)), *[dma((1,))] * 4, *[dma((3,))] * 4, dma((2,)), dma((2,)),
        dma((CHUNKS,)), dma((CHUNKS,)), dma((4, CHUNKS, 2)), dma((4, CHUNKS, 2)),
        dma((3,)), dma((3,)),
    ]
    grad_features, grad_weight = pl.pallas_call(
        body,
        out_shape=(
            jax.ShapeDtypeStruct((chan, tok), BF16),
            jax.ShapeDtypeStruct((group, chan), F32),
        ),
        in_specs=[pl.BlockSpec(memory_space=pltpu.HBM)] * 5,
        out_specs=(pl.BlockSpec(memory_space=pltpu.VMEM),) * 2,
        scratch_shapes=scratch,
        name="mixer",
        compiler_params=pltpu.CompilerParams(
            collective_id=0, has_side_effects=True, vmem_limit_bytes=60 << 20
        ),
    )(features, cotangent, blocks, twiddles, channel_weight)
    return grad_features, grad_weight.T


def solution(mesh):
    return jax.shard_map(
        per_device,
        mesh=mesh,
        in_specs=(
            P("ch", "rows"),
            P("ch", "rows"),
            P("rows", None, None),
            P(None, None, "rows"),
            P("ch", None),
        ),
        out_specs=(P("ch", "rows"), P("ch", "rows")),
        check_vma=False,
    )
```

```python
import jax
import jax.numpy as jnp
from jax import lax
from jax.experimental import pallas as pl
from jax.experimental.pallas import tpu as pltpu
from jax.sharding import PartitionSpec as P

MESH = pl.DeviceIdType.MESH
F32 = jnp.float32
BF16 = jnp.bfloat16

NX, NZ, NC, NY = 4, 4, 2, 4
ROWS = NX * NZ * NC
NB = NZ * NC
CHS = 2 * NY
BLK = 128
LOCAL = 3
LEVELS = 8
CROSS = LEVELS - LOCAL
CHUNKS = NZ
PARTS = 2
TILE = 16


def gelu_parts(v):
    half = 0.5 * (1.0 + lax.erf(v * 0.7071067811865476))
    act = v * half
    slope = half + v * jnp.exp(-0.5 * v * v) * 0.3989422804014327
    return act, slope


def flip(v, dist):
    n = v.shape[0]
    h = v.reshape((n // (2 * dist), 2, dist) + v.shape[1:])
    h = jnp.concatenate([h[:, 1:], h[:, :1]], axis=1)
    return h.reshape(v.shape)


def span(start, size):
    return pl.ds(pl.multiple_of(start, size), size)


def body(
    feat_hbm, cot_hbm, blocks_hbm, tw_hbm, w_hbm,
    gf_hbm, gw_hbm,
    feat, blocks, tw, w, cot,
    twst, twz, twall, twb, twl, m0, act, slope,
    s1, r1, s2, s3, r3, s4, r4, bk,
    gst, rc, p1, rx, p2, rz, gf_ref, gw_ref, out_sem,
    loc_sem, snd0, snd1, snd2, snd3, rcv0, rcv1, rcv2, rcv3, tw_send, tw_recv,
    cz_send, cz_recv, cy_send, cy_recv, g_send, g_recv,
):
    a2a_send, a2a_recv = (snd0, snd1, snd2, snd3), (rcv0, rcv1, rcv2, rcv3)
    row = lax.axis_index("rows")
    col = lax.axis_index("ch")
    x, zl, c = row // NB, (row // NC) % NZ, row % NC
    y, zh = col // 2, col % 2
    zc = row % NB
    up = {"ch": ((y + 1) % NY) * 2 + zh}
    down = {"ch": ((y + NY - 1) % NY) * 2 + zh}
    across = {"ch": y * 2 + (1 - zh)}
    chan, tok = feat.shape
    quarter = chan // NX
    tiles = quarter // TILE
    size = tok // CHUNKS
    group = gw_ref.shape[0]

    loads = [
        pltpu.make_async_copy(cot_hbm, cot.at[col], loc_sem.at[0]),
        pltpu.make_async_copy(tw_hbm, tw, loc_sem.at[1]),
        pltpu.make_async_copy(feat_hbm, feat, loc_sem.at[2]),
        pltpu.make_async_copy(blocks_hbm, blocks, loc_sem.at[3]),
        pltpu.make_async_copy(w_hbm, w, loc_sem.at[4]),
    ]
    for load in loads:
        load.start()

    bar = pltpu.get_barrier_semaphore()

    def greet(i, carry):
        pl.semaphore_signal(bar, inc=1, device_id={"rows": (row + i) % ROWS}, device_id_type=MESH)
        return carry

    lax.fori_loop(1, ROWS, greet, 0)
    for peer in (up, down, across):
        pl.semaphore_signal(bar, inc=1, device_id=peer, device_id_type=MESH)

    def local_fwd(t):
        for g in range(NB):
            lanes = slice(g * BLK, (g + 1) * BLK)
            left = jnp.concatenate(
                [feat[span(q * quarter + t * TILE, TILE), lanes] for q in range(NX)], axis=0
            )
            m0[g] = lax.dot_general(
                left, blocks[g], (((1,), (1,)), ((), ())), preferred_element_type=F32
            )

        def local_one(q, carry):
            v = m0[:, span(q * TILE, TILE), :].reshape(NB, 2, 8, BLK)
            for j in range(LOCAL):
                v = v * twl[0, j][:, None] + flip(v, 2**j) * twl[1, j][:, None]
            s1[q, :, span(t * TILE, TILE), :] = v.reshape(NB, TILE, BLK).astype(BF16)
            return carry

        lax.fori_loop(0, NX, local_one, 0)

    loads[1].wait()
    for b in range(NB):
        lanes = slice(b * BLK, (b + 1) * BLK)
        twst[b] = tw[:, :, lanes].reshape(2 * LEVELS, BLK).astype(BF16)

    loads[0].wait()
    pl.semaphore_wait(bar, ROWS - 1 + 3)

    def twz_send(i, carry):
        other = (zc + i) % NB
        pltpu.make_async_remote_copy(
            src_ref=twst.at[other], dst_ref=twz.at[zc],
            send_sem=tw_send.at[0], recv_sem=tw_recv.at[0],
            device_id={"rows": x * NB + other}, device_id_type=MESH,
        ).start()
        return carry

    lax.fori_loop(1, NB, twz_send, 0)
    pltpu.make_async_copy(twst.at[zc], twz.at[zc], tw_recv.at[0]).start()

    def exchange(step, t, src, dst, sem):
        part = span(t * TILE, TILE)

        def exch_one(i, carry):
            other = (row + i) % ROWS
            pltpu.make_async_remote_copy(
                src_ref=src.at[other // NB, other % NB, part], dst_ref=dst(row, part),
                send_sem=a2a_send[step].at[0], recv_sem=sem,
                device_id={"rows": other}, device_id_type=MESH,
            ).start()
            return carry

        lax.fori_loop(1, ROWS, exch_one, 0)
        pltpu.make_async_copy(src.at[x, zc, part], dst(row, part), sem).start()

    def slots(ref):
        return lambda r, part: ref.at[r // NB, r % NB, part]

    def arrived(step, t, ref):
        ref = ref.at[:, :, span(t * TILE, TILE)]
        pltpu.make_async_copy(ref, ref, a2a_recv[step].at[t]).wait()

    def chunk(k):
        return span(((zl + 1 + k) % NZ) * size, size)

    def cz(k):
        return pltpu.make_async_remote_copy(
            src_ref=cot.at[col, :, chunk(k)], dst_ref=cot.at[col, :, chunk(k)],
            send_sem=cz_send.at[k], recv_sem=cz_recv.at[k],
            device_id=across, device_id_type=MESH,
        )

    def cy(which, k, way, owner):
        return pltpu.make_async_remote_copy(
            src_ref=cot.at[owner, :, chunk(k)], dst_ref=cot.at[owner, :, chunk(k)],
            send_sem=cy_send.at[which, k, way], recv_sem=cy_recv.at[which, k, way],
            device_id=(up, down)[way], device_id_type=MESH,
        )

    sent = []

    def go(copy):
        copy.start()
        sent.append(copy)

    for k in range(CHUNKS):
        go(cz(k))
        for way in range(2):
            go(cy(0, k, way, col))

    for b in range(NB):
        lanes = slice(b * BLK, (b + 1) * BLK)
        for j in range(LOCAL):
            for s in range(2):
                twl[s, j, b] = jnp.broadcast_to(tw[s, j : j + 1, lanes], (8, BLK))

    loads[2].wait()
    loads[3].wait()
    for t in range(tiles):
        local_fwd(t)

    def relay(which, k):
        way = k % 2
        owner = ((y + NY - 1) % NY if way == 0 else (y + 1) % NY) * 2
        owner = owner + (zh if which == 0 else 1 - zh)
        cy(which, k, way, owner).wait_recv()
        go(cy(which + 1, k, way, owner))

    def far_send(k):
        cz(k).wait_recv()
        for way in range(2):
            go(cy(2, k, way, y * 2 + (1 - zh)))

    def spread(r, carry):
        u = twall[r // NB, r % NB].astype(F32)
        for j in range(CROSS):
            for s in range(2):
                at = s * LEVELS + LOCAL + j
                twb[s, j, r] = jnp.broadcast_to(u[at : at + 1, :], (8, BLK))
        return carry


    def cross_fwd(t):
        part = span(t * TILE, TILE)
        arrived(0, t, r1)
        v = r1[:, :, part, :].astype(F32).reshape(ROWS, 2, 8, BLK)
        for j in range(CROSS):
            v = v * twb[0, j][:, None] + flip(v, 2**j) * twb[1, j][:, None]
        slope[:, :, part, :] = v.reshape(NX, NB, TILE, BLK)

        def gelu_one(r, carry):
            a, s = gelu_parts(slope[r // NB, r % NB, part, :])
            s2[r // NB, r % NB, part, :] = a.astype(BF16)
            slope[r // NB, r % NB, part, :] = s
            return carry

        lax.fori_loop(0, ROWS, gelu_one, 0)
        exchange(
            1, t, s2,
            lambda r, _: act.at[span((r // NB) * quarter + t * TILE, TILE), span((r % NB) * BLK, BLK)],
            a2a_recv[1].at[0],
        )

    def project(k):
        way = k % 2
        for which in range(4):
            cy(which, k, way if which % 2 else 1 - way, col).wait_recv()
        piece = cot[:, :, chunk(k)].reshape(CHS * chan, size)
        back = jnp.dot(w[...], piece, preferred_element_type=F32).astype(BF16)
        first = ((zl + 1 + k) % NZ) * NC
        for q in range(NX):
            for j in range(NC):
                s3[q, first + j] = back[q * quarter : (q + 1) * quarter, j * BLK : (j + 1) * BLK]
        last = k == CHUNKS - 1
        for t in range(tiles):
            part = slice(t * TILE, (t + 1) * TILE)

            def a3_one(i, carry):
                at = (x * NC + c + i) % NB
                q, b = at // NC, first + at % NC
                pltpu.make_async_remote_copy(
                    src_ref=s3.at[q, b, part], dst_ref=r3.at[x, zc, part],
                    send_sem=a2a_send[2].at[0], recv_sem=a2a_recv[2].at[t],
                    device_id={"rows": q * NB + b}, device_id_type=MESH,
                ).start()
                return carry

            lax.fori_loop(1 if last else 0, NB, a3_one, 0)
            if last:
                pltpu.make_async_copy(
                    s3.at[x, zc, part], r3.at[x, zc, part], a2a_recv[2].at[t]
                ).start()

    relay(0, 0)
    pltpu.make_async_copy(twz, twz, tw_recv.at[0]).wait()

    def twx_send(i, carry):
        other = (x + i) % NX
        pltpu.make_async_remote_copy(
            src_ref=twz, dst_ref=twall.at[x],
            send_sem=tw_send.at[1], recv_sem=tw_recv.at[1],
            device_id={"rows": other * NB + zc}, device_id_type=MESH,
        ).start()
        return carry

    lax.fori_loop(1, NX, twx_send, 0)
    pltpu.make_async_copy(twz, twall.at[x], tw_recv.at[1]).start()

    relay(0, 1)
    far_send(0)
    for t in range(tiles):
        exchange(0, t, s1, slots(r1), a2a_recv[0].at[t])
    relay(0, 2)
    pltpu.make_async_copy(twall, twall, tw_recv.at[1]).wait()
    lax.fori_loop(0, ROWS, spread, 0)
    far_send(1)
    relay(2, 0)
    relay(0, 3)
    far_send(2)
    relay(2, 1)
    cross_fwd(0)
    far_send(3)
    relay(2, 2)
    cross_fwd(1)
    loads[4].wait()
    relay(2, 3)
    cross_fwd(2)
    project(0)
    project(1)
    project(2)
    project(3)

    def cross_bwd(t):
        part = span(t * TILE, TILE)
        arrived(2, t, r3)
        v = r3[:, :, part, :].astype(F32) * slope[:, :, part, :]
        v = v.reshape(ROWS, 2, 8, BLK)
        for j in reversed(range(CROSS)):
            v = v * twb[0, j][:, None] + flip(v * twb[1, j][:, None], 2**j)
        s4[:, :, part, :] = v.reshape(NX, NB, TILE, BLK).astype(BF16)
        exchange(3, t, s4, slots(r4), a2a_recv[3].at[t])

    written = []

    def local_bwd(t):
        arrived(3, t, r4)

        def bwd_one(q, carry):
            v = r4[q, :, span(t * TILE, TILE), :].astype(F32).reshape(NB, 2, 8, BLK)
            for j in reversed(range(LOCAL)):
                v = v * twl[0, j][:, None] + flip(v * twl[1, j][:, None], 2**j)
            bk[:, span(q * TILE, TILE), :] = v.reshape(NB, TILE, BLK).astype(BF16)
            return carry

        lax.fori_loop(0, NX, bwd_one, 0)
        for g in range(NB):
            out = jnp.dot(bk[g], blocks[g], preferred_element_type=F32).astype(BF16)
            for q in range(NX):
                gf_ref[span(q * quarter + t * TILE, TILE), g * BLK : (g + 1) * BLK] = out[
                    q * TILE : (q + 1) * TILE
                ]
        for q in range(NX):
            part = span(q * quarter + t * TILE, TILE)
            copy = pltpu.make_async_copy(gf_ref.at[part], gf_hbm.at[part], out_sem.at[t, q])
            copy.start()
            written.append(copy)

    pltpu.make_async_copy(act, act, a2a_recv[1].at[0]).wait()

    def weight(h, carry):
        g = lax.dot_general(
            cot[h], act[...], (((1,), (1,)), ((), ())), preferred_element_type=F32
        ).astype(BF16)
        for i in range(4):
            gst[i % 2, h // 2, (h % 2) * 2 + i // 2] = g[i * group : (i + 1) * group]
        return carry

    lax.fori_loop(0, CHS, weight, 0)
    g_core = pltpu.make_async_remote_copy(
        src_ref=gst.at[1 - c], dst_ref=rc, send_sem=g_send.at[0], recv_sem=g_recv.at[0],
        device_id={"rows": row + 1 - 2 * c}, device_id_type=MESH,
    )
    go(g_core)

    cross_bwd(0)

    g_core.wait_recv()
    for i in range(NX):
        p1[i] = (gst[c, i].astype(F32) + rc[i].astype(F32)).astype(BF16)

    def gx(i, carry):
        other = (x + i) % NX
        pltpu.make_async_remote_copy(
            src_ref=p1.at[other], dst_ref=rx.at[x], send_sem=g_send.at[1], recv_sem=g_recv.at[1],
            device_id={"rows": other * NB + zc}, device_id_type=MESH,
        ).start()
        return carry

    lax.fori_loop(1, NX, gx, 0)
    pltpu.make_async_copy(p1.at[x], rx.at[x], g_recv.at[1]).start()

    cross_bwd(1)

    cross_bwd(2)

    pltpu.make_async_copy(rx, rx, g_recv.at[1]).wait()
    for i in range(NZ):
        total = rx[0, i].astype(F32)
        for j in range(1, NX):
            total = total + rx[j, i].astype(F32)
        p2[i] = total.astype(BF16)

    def gz(i, carry):
        other = (zl + i) % NZ
        pltpu.make_async_remote_copy(
            src_ref=p2.at[other], dst_ref=rz.at[zl], send_sem=g_send.at[2], recv_sem=g_recv.at[2],
            device_id={"rows": x * NB + other * NC + c}, device_id_type=MESH,
        ).start()
        return carry

    lax.fori_loop(1, NZ, gz, 0)
    pltpu.make_async_copy(p2.at[zl], rz.at[zl], g_recv.at[2]).start()

    for t in range(tiles):
        local_bwd(t)

    pltpu.make_async_copy(rz, rz, g_recv.at[2]).wait()
    total = rz[0].astype(F32)
    for j in range(1, NZ):
        total = total + rz[j].astype(F32)
    gw_ref[...] = total * (1.0 / (tok * ROWS) ** 0.5)
    copy = pltpu.make_async_copy(gw_ref, gw_hbm, loc_sem.at[5])
    copy.start()
    written.append(copy)
    for copy in written:
        copy.wait()

    for step, src in enumerate((s1, s2, s3, s4)):
        for part in (src.at[0:3], src.at[3, 0:7]):
            pltpu.make_async_copy(part, part, a2a_send[step].at[0]).wait()
    pltpu.make_async_copy(twst.at[0:7], twst.at[0:7], tw_send.at[0]).wait()
    pltpu.make_async_copy(twall.at[0:3], twall.at[0:3], tw_send.at[1]).wait()
    for copy in sent:
        copy.wait_send()
    pltpu.make_async_copy(p1.at[0:3], p1.at[0:3], g_send.at[1]).wait()
    pltpu.make_async_copy(p2.at[0:3], p2.at[0:3], g_send.at[2]).wait()


def hand_over(gf_in, gw_in, gf_out, gw_out):
    gf_out[...] = gf_in[...]
    gw_out[...] = gw_in[...]


def per_device(features, cotangent, blocks, twiddles, channel_weight):
    chan, tok = features.shape
    quarter = chan // NX
    group = channel_weight.shape[1] // ROWS
    piece = (NX, NB, quarter, BLK)
    vm = pltpu.VMEM
    dma = pltpu.SemaphoreType.DMA
    scratch = [
        vm((chan, tok), BF16), vm(blocks.shape, BF16), vm(twiddles.shape, F32),
        vm(channel_weight.shape, BF16), vm((CHS, chan, tok), BF16),
        vm((NB, 2 * LEVELS, BLK), BF16), vm((NB, 2 * LEVELS, BLK), BF16),
        vm((NX, NB, 2 * LEVELS, BLK), BF16),
        vm((2, CROSS, ROWS, 8, BLK), F32), vm((2, LOCAL, NB, 8, BLK), F32),
        vm((NB, NX * TILE, BLK), F32), vm((chan, tok), BF16), vm(piece, F32),
        *[vm(piece, BF16)] * 7, vm((NB, NX * TILE, BLK), BF16),
        vm((NC, NX, NZ, group, chan), BF16), vm((NX, NZ, group, chan), BF16),
        vm((NX, NZ, group, chan), BF16), vm((NX, NZ, group, chan), BF16),
        vm((NZ, group, chan), BF16), vm((NZ, group, chan), BF16),
        vm((chan, tok), BF16), vm((group, chan), F32), dma((3, NX)),
        dma((6,)), *[dma((1,))] * 4, *[dma((3,))] * 4, dma((2,)), dma((2,)),
        dma((CHUNKS,)), dma((CHUNKS,)), dma((4, CHUNKS, 2)), dma((4, CHUNKS, 2)),
        dma((3,)), dma((3,)),
    ]
    grad_features, grad_weight = pl.pallas_call(
        body,
        out_shape=(
            jax.ShapeDtypeStruct((chan, tok), BF16),
            jax.ShapeDtypeStruct((group, chan), F32),
        ),
        in_specs=[pl.BlockSpec(memory_space=pltpu.HBM)] * 5,
        out_specs=(pl.BlockSpec(memory_space=pl.ANY),) * 2,
        scratch_shapes=scratch,
        name="mixer",
        compiler_params=pltpu.CompilerParams(
            collective_id=0, has_side_effects=True, vmem_limit_bytes=60 << 20
        ),
    )(features, cotangent, blocks, twiddles, channel_weight)
    steps = [
        pl.BlockSpec((chan // PARTS, tok), lambda i: (i, 0)),
        pl.BlockSpec((group, chan), lambda i: (0, 0)),
    ]
    grad_features, grad_weight = pl.pallas_call(
        hand_over,
        out_shape=(
            jax.ShapeDtypeStruct((chan, tok), BF16),
            jax.ShapeDtypeStruct((group, chan), F32),
        ),
        grid=(PARTS,),
        in_specs=steps,
        out_specs=steps,
        name="hand_over",
        compiler_params=pltpu.CompilerParams(vmem_limit_bytes=60 << 20),
    )(grad_features, grad_weight)
    return grad_features, grad_weight.T


def solution(mesh):
    return jax.shard_map(
        per_device,
        mesh=mesh,
        in_specs=(
            P("ch", "rows"),
            P("ch", "rows"),
            P("rows", None, None),
            P(None, None, "rows"),
            P("ch", None),
        ),
        out_specs=(P("ch", "rows"), P("ch", "rows")),
        check_vma=False,
    )
```

```python
import jax
import jax.numpy as jnp
from jax import lax
from jax.experimental import pallas as pl
from jax.experimental.pallas import tpu as pltpu
from jax.sharding import PartitionSpec as P

MESH = pl.DeviceIdType.MESH
F32 = jnp.float32
BF16 = jnp.bfloat16

NX, NZ, NC, NY = 4, 4, 2, 4
ROWS = NX * NZ * NC
NB = NZ * NC
CHS = 2 * NY
BLK = 128
LOCAL = 3
LEVELS = 8
CROSS = LEVELS - LOCAL
CHUNKS = NZ
PARTS = 2
TILE = 16


def gelu_parts(v):
    half = 0.5 * (1.0 + lax.erf(v * 0.7071067811865476))
    act = v * half
    slope = half + v * jnp.exp(-0.5 * v * v) * 0.3989422804014327
    return act, slope


def flip(v, dist):
    n = v.shape[0]
    h = v.reshape((n // (2 * dist), 2, dist) + v.shape[1:])
    h = jnp.concatenate([h[:, 1:], h[:, :1]], axis=1)
    return h.reshape(v.shape)


def span(start, size):
    return pl.ds(pl.multiple_of(start, size), size)


def body(
    feat_hbm, cot_hbm, blocks_hbm, tw_hbm, w_hbm,
    gf_hbm, gw_hbm,
    feat, blocks, tw, w, cot,
    twst, twz, twall, twb, twl, m0, act, slope,
    s1, r1, s2, s3, r3, s4, r4, bk,
    gst, rc, p1, rx, p2, rz, gf_ref, gw_ref, out_sem,
    loc_sem, snd0, snd1, snd2, snd3, rcv0, rcv1, rcv2, rcv3, tw_send, tw_recv,
    cz_send, cz_recv, cy_send, cy_recv, g_send, g_recv,
):
    a2a_send, a2a_recv = (snd0, snd1, snd2, snd3), (rcv0, rcv1, rcv2, rcv3)
    row = lax.axis_index("rows")
    col = lax.axis_index("ch")
    x, zl, c = row // NB, (row // NC) % NZ, row % NC
    y, zh = col // 2, col % 2
    zc = row % NB
    up = {"ch": ((y + 1) % NY) * 2 + zh}
    down = {"ch": ((y + NY - 1) % NY) * 2 + zh}
    across = {"ch": y * 2 + (1 - zh)}
    chan, tok = feat.shape
    quarter = chan // NX
    tiles = quarter // TILE
    size = tok // CHUNKS
    group = gw_ref.shape[0]

    loads = [
        pltpu.make_async_copy(cot_hbm, cot.at[col], loc_sem.at[0]),
        pltpu.make_async_copy(tw_hbm, tw, loc_sem.at[1]),
        pltpu.make_async_copy(feat_hbm, feat, loc_sem.at[2]),
        pltpu.make_async_copy(blocks_hbm, blocks, loc_sem.at[3]),
        pltpu.make_async_copy(w_hbm, w, loc_sem.at[4]),
    ]
    for load in loads:
        load.start()

    bar = pltpu.get_barrier_semaphore()

    def greet(i, carry):
        pl.semaphore_signal(bar, inc=1, device_id={"rows": (row + i) % ROWS}, device_id_type=MESH)
        return carry

    lax.fori_loop(1, ROWS, greet, 0)
    for peer in (up, down, across):
        pl.semaphore_signal(bar, inc=1, device_id=peer, device_id_type=MESH)

    def local_fwd(t):
        for g in range(NB):
            lanes = slice(g * BLK, (g + 1) * BLK)
            left = jnp.concatenate(
                [feat[span(q * quarter + t * TILE, TILE), lanes] for q in range(NX)], axis=0
            )
            m0[g] = lax.dot_general(
                left, blocks[g], (((1,), (1,)), ((), ())), preferred_element_type=F32
            )

        def local_one(q, carry):
            v = m0[:, span(q * TILE, TILE), :].reshape(NB, 2, 8, BLK)
            for j in range(LOCAL):
                v = v * twl[0, j][:, None] + flip(v, 2**j) * twl[1, j][:, None]
            s1[q, :, span(t * TILE, TILE), :] = v.reshape(NB, TILE, BLK).astype(BF16)
            return carry

        lax.fori_loop(0, NX, local_one, 0)

    loads[1].wait()
    for b in range(NB):
        lanes = slice(b * BLK, (b + 1) * BLK)
        twst[b] = tw[:, :, lanes].reshape(2 * LEVELS, BLK).astype(BF16)

    loads[0].wait()
    pl.semaphore_wait(bar, ROWS - 1 + 3)

    def twz_send(i, carry):
        other = (zc + i) % NB
        pltpu.make_async_remote_copy(
            src_ref=twst.at[other], dst_ref=twz.at[zc],
            send_sem=tw_send.at[0], recv_sem=tw_recv.at[0],
            device_id={"rows": x * NB + other}, device_id_type=MESH,
        ).start()
        return carry

    lax.fori_loop(1, NB, twz_send, 0)
    pltpu.make_async_copy(twst.at[zc], twz.at[zc], tw_recv.at[0]).start()

    def exchange(step, t, src, dst, sem):
        part = span(t * TILE, TILE)

        def exch_one(i, carry):
            other = (row + i) % ROWS
            pltpu.make_async_remote_copy(
                src_ref=src.at[other // NB, other % NB, part], dst_ref=dst(row, part),
                send_sem=a2a_send[step].at[0], recv_sem=sem,
                device_id={"rows": other}, device_id_type=MESH,
            ).start()
            return carry

        lax.fori_loop(1, ROWS, exch_one, 0)
        pltpu.make_async_copy(src.at[x, zc, part], dst(row, part), sem).start()

    def slots(ref):
        return lambda r, part: ref.at[r // NB, r % NB, part]

    def arrived(step, t, ref):
        ref = ref.at[:, :, span(t * TILE, TILE)]
        pltpu.make_async_copy(ref, ref, a2a_recv[step].at[t]).wait()

    def chunk(k):
        return span(((zl + 1 + k) % NZ) * size, size)

    def cz(k):
        return pltpu.make_async_remote_copy(
            src_ref=cot.at[col, :, chunk(k)], dst_ref=cot.at[col, :, chunk(k)],
            send_sem=cz_send.at[k], recv_sem=cz_recv.at[k],
            device_id=across, device_id_type=MESH,
        )

    def cy(which, k, way, owner):
        return pltpu.make_async_remote_copy(
            src_ref=cot.at[owner, :, chunk(k)], dst_ref=cot.at[owner, :, chunk(k)],
            send_sem=cy_send.at[which, k, way], recv_sem=cy_recv.at[which, k, way],
            device_id=(up, down)[way], device_id_type=MESH,
        )

    sent = []

    def go(copy):
        copy.start()
        sent.append(copy)

    for k in range(CHUNKS):
        go(cz(k))
        for way in range(2):
            go(cy(0, k, way, col))

    for b in range(NB):
        lanes = slice(b * BLK, (b + 1) * BLK)
        for j in range(LOCAL):
            for s in range(2):
                twl[s, j, b] = jnp.broadcast_to(tw[s, j : j + 1, lanes], (8, BLK))

    loads[2].wait()
    loads[3].wait()
    for t in range(tiles):
        local_fwd(t)

    def relay(which, k):
        way = k % 2
        owner = ((y + NY - 1) % NY if way == 0 else (y + 1) % NY) * 2
        owner = owner + (zh if which == 0 else 1 - zh)
        cy(which, k, way, owner).wait_recv()
        go(cy(which + 1, k, way, owner))

    def far_send(k):
        cz(k).wait_recv()
        for way in range(2):
            go(cy(2, k, way, y * 2 + (1 - zh)))

    def spread(r, carry):
        u = twall[r // NB, r % NB].astype(F32)
        for j in range(CROSS):
            for s in range(2):
                at = s * LEVELS + LOCAL + j
                twb[s, j, r] = jnp.broadcast_to(u[at : at + 1, :], (8, BLK))
        return carry


    def cross_fwd(t):
        part = span(t * TILE, TILE)
        arrived(0, t, r1)
        v = r1[:, :, part, :].astype(F32).reshape(ROWS, 2, 8, BLK)
        for j in range(CROSS):
            v = v * twb[0, j][:, None] + flip(v, 2**j) * twb[1, j][:, None]
        slope[:, :, part, :] = v.reshape(NX, NB, TILE, BLK)

        def gelu_one(r, carry):
            a, s = gelu_parts(slope[r // NB, r % NB, part, :])
            s2[r // NB, r % NB, part, :] = a.astype(BF16)
            slope[r // NB, r % NB, part, :] = s
            return carry

        lax.fori_loop(0, ROWS, gelu_one, 0)
        exchange(
            1, t, s2,
            lambda r, _: act.at[span((r // NB) * quarter + t * TILE, TILE), span((r % NB) * BLK, BLK)],
            a2a_recv[1].at[0],
        )

    def project(k):
        way = k % 2
        for which in range(4):
            cy(which, k, way if which % 2 else 1 - way, col).wait_recv()
        piece = cot[:, :, chunk(k)].reshape(CHS * chan, size)
        back = jnp.dot(w[...], piece, preferred_element_type=F32).astype(BF16)
        first = ((zl + 1 + k) % NZ) * NC
        for q in range(NX):
            for j in range(NC):
                s3[q, first + j] = back[q * quarter : (q + 1) * quarter, j * BLK : (j + 1) * BLK]
        last = k == CHUNKS - 1
        for t in range(tiles):
            part = slice(t * TILE, (t + 1) * TILE)

            def a3_one(i, carry):
                at = (x * NC + c + i) % NB
                q, b = at // NC, first + at % NC
                pltpu.make_async_remote_copy(
                    src_ref=s3.at[q, b, part], dst_ref=r3.at[x, zc, part],
                    send_sem=a2a_send[2].at[0], recv_sem=a2a_recv[2].at[t],
                    device_id={"rows": q * NB + b}, device_id_type=MESH,
                ).start()
                return carry

            lax.fori_loop(1 if last else 0, NB, a3_one, 0)
            if last:
                pltpu.make_async_copy(
                    s3.at[x, zc, part], r3.at[x, zc, part], a2a_recv[2].at[t]
                ).start()

    relay(0, 0)
    pltpu.make_async_copy(twz, twz, tw_recv.at[0]).wait()

    def twx_send(i, carry):
        other = (x + i) % NX
        pltpu.make_async_remote_copy(
            src_ref=twz, dst_ref=twall.at[x],
            send_sem=tw_send.at[1], recv_sem=tw_recv.at[1],
            device_id={"rows": other * NB + zc}, device_id_type=MESH,
        ).start()
        return carry

    lax.fori_loop(1, NX, twx_send, 0)
    pltpu.make_async_copy(twz, twall.at[x], tw_recv.at[1]).start()

    relay(0, 1)
    far_send(0)
    for t in range(tiles):
        exchange(0, t, s1, slots(r1), a2a_recv[0].at[t])
    relay(0, 2)
    pltpu.make_async_copy(twall, twall, tw_recv.at[1]).wait()
    lax.fori_loop(0, ROWS, spread, 0)
    far_send(1)
    relay(2, 0)
    relay(0, 3)
    far_send(2)
    relay(2, 1)
    cross_fwd(0)
    far_send(3)
    relay(2, 2)
    cross_fwd(1)
    loads[4].wait()
    relay(2, 3)
    cross_fwd(2)
    project(0)
    project(1)
    project(2)
    project(3)

    def cross_bwd(t):
        part = span(t * TILE, TILE)
        arrived(2, t, r3)
        v = r3[:, :, part, :].astype(F32) * slope[:, :, part, :]
        v = v.reshape(ROWS, 2, 8, BLK)
        for j in reversed(range(CROSS)):
            v = v * twb[0, j][:, None] + flip(v * twb[1, j][:, None], 2**j)
        s4[:, :, part, :] = v.reshape(NX, NB, TILE, BLK).astype(BF16)
        exchange(3, t, s4, slots(r4), a2a_recv[3].at[t])

    written = []

    def local_bwd(t):
        arrived(3, t, r4)

        def bwd_one(q, carry):
            v = r4[q, :, span(t * TILE, TILE), :].astype(F32).reshape(NB, 2, 8, BLK)
            for j in reversed(range(LOCAL)):
                v = v * twl[0, j][:, None] + flip(v * twl[1, j][:, None], 2**j)
            bk[:, span(q * TILE, TILE), :] = v.reshape(NB, TILE, BLK).astype(BF16)
            return carry

        lax.fori_loop(0, NX, bwd_one, 0)
        for g in range(NB):
            out = jnp.dot(bk[g], blocks[g], preferred_element_type=F32).astype(BF16)
            for q in range(NX):
                gf_ref[span(q * quarter + t * TILE, TILE), g * BLK : (g + 1) * BLK] = out[
                    q * TILE : (q + 1) * TILE
                ]
        for q in range(NX):
            part = span(q * quarter + t * TILE, TILE)
            copy = pltpu.make_async_copy(gf_ref.at[part], gf_hbm.at[part], out_sem.at[t, q])
            copy.start()
            written.append(copy)

    pltpu.make_async_copy(act, act, a2a_recv[1].at[0]).wait()

    def weight(h, carry):
        g = lax.dot_general(
            cot[h], act[...], (((1,), (1,)), ((), ())), preferred_element_type=F32
        ).astype(BF16)
        for i in range(4):
            gst[i % 2, h // 2, (h % 2) * 2 + i // 2] = g[i * group : (i + 1) * group]
        return carry

    for i in range(NX):
        lax.fori_loop(2 * i, 2 * i + 2, weight, 0)
        pltpu.make_async_remote_copy(
            src_ref=gst.at[1 - c, i], dst_ref=rc.at[i],
            send_sem=g_send.at[0], recv_sem=g_recv.at[0],
            device_id={"rows": row + 1 - 2 * c}, device_id_type=MESH,
        ).start()

    cross_bwd(0)

    pltpu.make_async_copy(rc, rc, g_recv.at[0]).wait()
    for i in range(NX):
        p1[i] = (gst[c, i].astype(F32) + rc[i].astype(F32)).astype(BF16)

    def gx(i, carry):
        other = (x + i) % NX
        pltpu.make_async_remote_copy(
            src_ref=p1.at[other], dst_ref=rx.at[x], send_sem=g_send.at[1], recv_sem=g_recv.at[1],
            device_id={"rows": other * NB + zc}, device_id_type=MESH,
        ).start()
        return carry

    lax.fori_loop(1, NX, gx, 0)
    pltpu.make_async_copy(p1.at[x], rx.at[x], g_recv.at[1]).start()

    cross_bwd(1)

    cross_bwd(2)

    pltpu.make_async_copy(rx, rx, g_recv.at[1]).wait()
    for i in range(NZ):
        total = rx[0, i].astype(F32)
        for j in range(1, NX):
            total = total + rx[j, i].astype(F32)
        p2[i] = total.astype(BF16)

    def gz(i, carry):
        other = (zl + i) % NZ
        pltpu.make_async_remote_copy(
            src_ref=p2.at[other], dst_ref=rz.at[zl], send_sem=g_send.at[2], recv_sem=g_recv.at[2],
            device_id={"rows": x * NB + other * NC + c}, device_id_type=MESH,
        ).start()
        return carry

    lax.fori_loop(1, NZ, gz, 0)
    pltpu.make_async_copy(p2.at[zl], rz.at[zl], g_recv.at[2]).start()

    for t in range(tiles):
        local_bwd(t)

    pltpu.make_async_copy(rz, rz, g_recv.at[2]).wait()
    total = rz[0].astype(F32)
    for j in range(1, NZ):
        total = total + rz[j].astype(F32)
    gw_ref[...] = total * (1.0 / (tok * ROWS) ** 0.5)
    copy = pltpu.make_async_copy(gw_ref, gw_hbm, loc_sem.at[5])
    copy.start()
    written.append(copy)
    for copy in written:
        copy.wait()

    for step, src in enumerate((s1, s2, s3, s4)):
        for part in (src.at[0:3], src.at[3, 0:7]):
            pltpu.make_async_copy(part, part, a2a_send[step].at[0]).wait()
    pltpu.make_async_copy(twst.at[0:7], twst.at[0:7], tw_send.at[0]).wait()
    pltpu.make_async_copy(twall.at[0:3], twall.at[0:3], tw_send.at[1]).wait()
    for copy in sent:
        copy.wait_send()
    pltpu.make_async_copy(rc, rc, g_send.at[0]).wait()
    pltpu.make_async_copy(p1.at[0:3], p1.at[0:3], g_send.at[1]).wait()
    pltpu.make_async_copy(p2.at[0:3], p2.at[0:3], g_send.at[2]).wait()


def hand_over(gf_in, gw_in, gf_out, gw_out):
    gf_out[...] = gf_in[...]
    gw_out[...] = gw_in[...]


def per_device(features, cotangent, blocks, twiddles, channel_weight):
    chan, tok = features.shape
    quarter = chan // NX
    group = channel_weight.shape[1] // ROWS
    piece = (NX, NB, quarter, BLK)
    vm = pltpu.VMEM
    dma = pltpu.SemaphoreType.DMA
    scratch = [
        vm((chan, tok), BF16), vm(blocks.shape, BF16), vm(twiddles.shape, F32),
        vm(channel_weight.shape, BF16), vm((CHS, chan, tok), BF16),
        vm((NB, 2 * LEVELS, BLK), BF16), vm((NB, 2 * LEVELS, BLK), BF16),
        vm((NX, NB, 2 * LEVELS, BLK), BF16),
        vm((2, CROSS, ROWS, 8, BLK), F32), vm((2, LOCAL, NB, 8, BLK), F32),
        vm((NB, NX * TILE, BLK), F32), vm((chan, tok), BF16), vm(piece, F32),
        *[vm(piece, BF16)] * 7, vm((NB, NX * TILE, BLK), BF16),
        vm((NC, NX, NZ, group, chan), BF16), vm((NX, NZ, group, chan), BF16),
        vm((NX, NZ, group, chan), BF16), vm((NX, NZ, group, chan), BF16),
        vm((NZ, group, chan), BF16), vm((NZ, group, chan), BF16),
        vm((chan, tok), BF16), vm((group, chan), F32), dma((3, NX)),
        dma((6,)), *[dma((1,))] * 4, *[dma((3,))] * 4, dma((2,)), dma((2,)),
        dma((CHUNKS,)), dma((CHUNKS,)), dma((4, CHUNKS, 2)), dma((4, CHUNKS, 2)),
        dma((3,)), dma((3,)),
    ]
    grad_features, grad_weight = pl.pallas_call(
        body,
        out_shape=(
            jax.ShapeDtypeStruct((chan, tok), BF16),
            jax.ShapeDtypeStruct((group, chan), F32),
        ),
        in_specs=[pl.BlockSpec(memory_space=pltpu.HBM)] * 5,
        out_specs=(pl.BlockSpec(memory_space=pl.ANY),) * 2,
        scratch_shapes=scratch,
        name="mixer",
        compiler_params=pltpu.CompilerParams(
            collective_id=0, has_side_effects=True, vmem_limit_bytes=60 << 20
        ),
    )(features, cotangent, blocks, twiddles, channel_weight)
    steps = [
        pl.BlockSpec((chan // PARTS, tok), lambda i: (i, 0)),
        pl.BlockSpec((group, chan), lambda i: (0, 0)),
    ]
    grad_features, grad_weight = pl.pallas_call(
        hand_over,
        out_shape=(
            jax.ShapeDtypeStruct((chan, tok), BF16),
            jax.ShapeDtypeStruct((group, chan), F32),
        ),
        grid=(PARTS,),
        in_specs=steps,
        out_specs=steps,
        name="hand_over",
        compiler_params=pltpu.CompilerParams(vmem_limit_bytes=60 << 20),
    )(grad_features, grad_weight)
    return grad_features, grad_weight.T


def solution(mesh):
    return jax.shard_map(
        per_device,
        mesh=mesh,
        in_specs=(
            P("ch", "rows"),
            P("ch", "rows"),
            P("rows", None, None),
            P(None, None, "rows"),
            P("ch", None),
        ),
        out_specs=(P("ch", "rows"), P("ch", "rows")),
        check_vma=False,
    )
```

```python
import jax
import jax.numpy as jnp
from jax import lax
from jax.experimental import pallas as pl
from jax.experimental.pallas import tpu as pltpu
from jax.sharding import PartitionSpec as P

MESH = pl.DeviceIdType.MESH
F32 = jnp.float32
BF16 = jnp.bfloat16

NX, NZ, NC, NY = 4, 4, 2, 4
ROWS = NX * NZ * NC
NB = NZ * NC
CHS = 2 * NY
BLK = 128
LOCAL = 3
LEVELS = 8
CROSS = LEVELS - LOCAL
CHUNKS = NZ
PARTS = 2
TILE = 16


def gelu_parts(v):
    half = 0.5 * (1.0 + lax.erf(v * 0.7071067811865476))
    act = v * half
    slope = half + v * jnp.exp(-0.5 * v * v) * 0.3989422804014327
    return act, slope


def flip(v, dist):
    n = v.shape[0]
    h = v.reshape((n // (2 * dist), 2, dist) + v.shape[1:])
    h = jnp.concatenate([h[:, 1:], h[:, :1]], axis=1)
    return h.reshape(v.shape)


def span(start, size):
    return pl.ds(pl.multiple_of(start, size), size)


def body(
    feat_hbm, cot_hbm, blocks_hbm, tw_hbm, w_hbm,
    gf_hbm, gw_hbm,
    feat, blocks, tw, w, cot,
    twst, twz, twall, twb, twl, m0, act, slope,
    s1, r1, s2, s3, r3, s4, r4, bk,
    gst, rc, p1, rx, p2, rz, gf_ref, gw_ref, out_sem,
    loc_sem, snd0, snd1, snd2, snd3, rcv0, rcv1, rcv2, rcv3, tw_send, tw_recv,
    cz_send, cz_recv, cy_send, cy_recv, g_send, g_recv,
):
    a2a_send, a2a_recv = (snd0, snd1, snd2, snd3), (rcv0, rcv1, rcv2, rcv3)
    row = lax.axis_index("rows")
    col = lax.axis_index("ch")
    x, zl, c = row // NB, (row // NC) % NZ, row % NC
    y, zh = col // 2, col % 2
    zc = row % NB
    up = {"ch": ((y + 1) % NY) * 2 + zh}
    down = {"ch": ((y + NY - 1) % NY) * 2 + zh}
    across = {"ch": y * 2 + (1 - zh)}
    chan, tok = feat.shape
    quarter = chan // NX
    tiles = quarter // TILE
    size = tok // CHUNKS
    group = gw_ref.shape[0]

    loads = [
        pltpu.make_async_copy(cot_hbm, cot.at[col], loc_sem.at[0]),
        pltpu.make_async_copy(tw_hbm, tw, loc_sem.at[1]),
        pltpu.make_async_copy(feat_hbm, feat, loc_sem.at[2]),
        pltpu.make_async_copy(blocks_hbm, blocks, loc_sem.at[3]),
        pltpu.make_async_copy(w_hbm, w, loc_sem.at[4]),
    ]
    for load in loads:
        load.start()

    bar = pltpu.get_barrier_semaphore()

    def greet(i, carry):
        pl.semaphore_signal(bar, inc=1, device_id={"rows": (row + i) % ROWS}, device_id_type=MESH)
        return carry

    lax.fori_loop(1, ROWS, greet, 0)
    for peer in (up, down, across):
        pl.semaphore_signal(bar, inc=1, device_id=peer, device_id_type=MESH)

    def local_fwd(t):
        for g in range(NB):
            lanes = slice(g * BLK, (g + 1) * BLK)
            left = jnp.concatenate(
                [feat[span(q * quarter + t * TILE, TILE), lanes] for q in range(NX)], axis=0
            )
            m0[g] = lax.dot_general(
                left, blocks[g], (((1,), (1,)), ((), ())), preferred_element_type=F32
            )

        def local_one(q, carry):
            v = m0[:, span(q * TILE, TILE), :].reshape(NB, 2, 8, BLK)
            for j in range(LOCAL):
                v = v * twl[0, j][:, None] + flip(v, 2**j) * twl[1, j][:, None]
            s1[q, :, span(t * TILE, TILE), :] = v.reshape(NB, TILE, BLK).astype(BF16)
            return carry

        lax.fori_loop(0, NX, local_one, 0)

    loads[1].wait()
    for b in range(NB):
        lanes = slice(b * BLK, (b + 1) * BLK)
        twst[b] = tw[:, :, lanes].reshape(2 * LEVELS, BLK).astype(BF16)

    loads[0].wait()
    pl.semaphore_wait(bar, ROWS - 1 + 3)

    def twz_send(i, carry):
        other = (zc + i) % NB
        pltpu.make_async_remote_copy(
            src_ref=twst.at[other], dst_ref=twz.at[zc],
            send_sem=tw_send.at[0], recv_sem=tw_recv.at[0],
            device_id={"rows": x * NB + other}, device_id_type=MESH,
        ).start()
        return carry

    lax.fori_loop(1, NB, twz_send, 0)
    pltpu.make_async_copy(twst.at[zc], twz.at[zc], tw_recv.at[0]).start()

    def exchange(step, t, src, dst, sem):
        part = span(t * TILE, TILE)

        def exch_one(i, carry):
            other = (row + i) % ROWS
            pltpu.make_async_remote_copy(
                src_ref=src.at[other // NB, other % NB, part], dst_ref=dst(row, part),
                send_sem=a2a_send[step].at[0], recv_sem=sem,
                device_id={"rows": other}, device_id_type=MESH,
            ).start()
            return carry

        lax.fori_loop(1, ROWS, exch_one, 0)
        pltpu.make_async_copy(src.at[x, zc, part], dst(row, part), sem).start()

    def slots(ref):
        return lambda r, part: ref.at[r // NB, r % NB, part]

    def arrived(step, t, ref):
        ref = ref.at[:, :, span(t * TILE, TILE)]
        pltpu.make_async_copy(ref, ref, a2a_recv[step].at[t]).wait()

    def chunk(k):
        return span(((zl + 1 + k) % NZ) * size, size)

    def cz(k):
        return pltpu.make_async_remote_copy(
            src_ref=cot.at[col, :, chunk(k)], dst_ref=cot.at[col, :, chunk(k)],
            send_sem=cz_send.at[k], recv_sem=cz_recv.at[k],
            device_id=across, device_id_type=MESH,
        )

    def cy(which, k, way, owner):
        return pltpu.make_async_remote_copy(
            src_ref=cot.at[owner, :, chunk(k)], dst_ref=cot.at[owner, :, chunk(k)],
            send_sem=cy_send.at[which, k, way], recv_sem=cy_recv.at[which, k, way],
            device_id=(up, down)[way], device_id_type=MESH,
        )

    sent = []

    def go(copy):
        copy.start()
        sent.append(copy)

    for k in range(CHUNKS):
        go(cz(k))
        for way in range(2):
            go(cy(0, k, way, col))

    for b in range(NB):
        lanes = slice(b * BLK, (b + 1) * BLK)
        for j in range(LOCAL):
            for s in range(2):
                twl[s, j, b] = jnp.broadcast_to(tw[s, j : j + 1, lanes], (8, BLK))

    loads[2].wait()
    loads[3].wait()
    for t in range(tiles):
        local_fwd(t)

    def relay(which, k):
        way = k % 2
        owner = ((y + NY - 1) % NY if way == 0 else (y + 1) % NY) * 2
        owner = owner + (zh if which == 0 else 1 - zh)
        cy(which, k, way, owner).wait_recv()
        go(cy(which + 1, k, way, owner))

    def far_send(k):
        cz(k).wait_recv()
        for way in range(2):
            go(cy(2, k, way, y * 2 + (1 - zh)))

    def spread(r, carry):
        u = twall[r // NB, r % NB].astype(F32)
        for j in range(CROSS):
            for s in range(2):
                at = s * LEVELS + LOCAL + j
                twb[s, j, r] = jnp.broadcast_to(u[at : at + 1, :], (8, BLK))
        return carry


    def cross_fwd(t):
        part = span(t * TILE, TILE)
        arrived(0, t, r1)
        v = r1[:, :, part, :].astype(F32).reshape(ROWS, 2, 8, BLK)
        for j in range(CROSS):
            v = v * twb[0, j][:, None] + flip(v, 2**j) * twb[1, j][:, None]
        slope[:, :, part, :] = v.reshape(NX, NB, TILE, BLK)

        def gelu_one(i, carry):
            q, b = i // 2, (i % 2) * 4
            a, slant = gelu_parts(slope[q, pl.ds(b, 4), part, :])
            s2[q, pl.ds(b, 4), part, :] = a.astype(BF16)
            slope[q, pl.ds(b, 4), part, :] = slant
            return carry

        lax.fori_loop(0, NX * 2, gelu_one, 0)
        exchange(
            1, t, s2,
            lambda r, _: act.at[span((r // NB) * quarter + t * TILE, TILE), span((r % NB) * BLK, BLK)],
            a2a_recv[1].at[0],
        )

    def project(k):
        way = k % 2
        for which in range(4):
            cy(which, k, way if which % 2 else 1 - way, col).wait_recv()
        piece = cot[:, :, chunk(k)].reshape(CHS * chan, size)
        back = jnp.dot(w[...], piece, preferred_element_type=F32).astype(BF16)
        first = ((zl + 1 + k) % NZ) * NC
        for q in range(NX):
            for j in range(NC):
                s3[q, first + j] = back[q * quarter : (q + 1) * quarter, j * BLK : (j + 1) * BLK]
        last = k == CHUNKS - 1
        for t in range(tiles):
            part = slice(t * TILE, (t + 1) * TILE)

            def a3_one(i, carry):
                at = (x * NC + c + i) % NB
                q, b = at // NC, first + at % NC
                pltpu.make_async_remote_copy(
                    src_ref=s3.at[q, b, part], dst_ref=r3.at[x, zc, part],
                    send_sem=a2a_send[2].at[0], recv_sem=a2a_recv[2].at[t],
                    device_id={"rows": q * NB + b}, device_id_type=MESH,
                ).start()
                return carry

            lax.fori_loop(1 if last else 0, NB, a3_one, 0)
            if last:
                pltpu.make_async_copy(
                    s3.at[x, zc, part], r3.at[x, zc, part], a2a_recv[2].at[t]
                ).start()

    relay(0, 0)
    pltpu.make_async_copy(twz, twz, tw_recv.at[0]).wait()

    def twx_send(i, carry):
        other = (x + i) % NX
        pltpu.make_async_remote_copy(
            src_ref=twz, dst_ref=twall.at[x],
            send_sem=tw_send.at[1], recv_sem=tw_recv.at[1],
            device_id={"rows": other * NB + zc}, device_id_type=MESH,
        ).start()
        return carry

    lax.fori_loop(1, NX, twx_send, 0)
    pltpu.make_async_copy(twz, twall.at[x], tw_recv.at[1]).start()

    relay(0, 1)
    far_send(0)
    for t in range(tiles):
        exchange(0, t, s1, slots(r1), a2a_recv[0].at[t])
    relay(0, 2)
    pltpu.make_async_copy(twall, twall, tw_recv.at[1]).wait()
    lax.fori_loop(0, ROWS, spread, 0)
    far_send(1)
    relay(2, 0)
    relay(0, 3)
    far_send(2)
    relay(2, 1)
    cross_fwd(0)
    far_send(3)
    relay(2, 2)
    cross_fwd(1)
    loads[4].wait()
    relay(2, 3)
    cross_fwd(2)
    project(0)
    project(1)
    project(2)
    project(3)

    def cross_bwd(t):
        part = span(t * TILE, TILE)
        arrived(2, t, r3)
        v = r3[:, :, part, :].astype(F32) * slope[:, :, part, :]
        v = v.reshape(ROWS, 2, 8, BLK)
        for j in reversed(range(CROSS)):
            v = v * twb[0, j][:, None] + flip(v * twb[1, j][:, None], 2**j)
        s4[:, :, part, :] = v.reshape(NX, NB, TILE, BLK).astype(BF16)
        exchange(3, t, s4, slots(r4), a2a_recv[3].at[t])

    written = []

    def local_bwd(t):
        arrived(3, t, r4)

        def bwd_one(q, carry):
            v = r4[q, :, span(t * TILE, TILE), :].astype(F32).reshape(NB, 2, 8, BLK)
            for j in reversed(range(LOCAL)):
                v = v * twl[0, j][:, None] + flip(v * twl[1, j][:, None], 2**j)
            bk[:, span(q * TILE, TILE), :] = v.reshape(NB, TILE, BLK).astype(BF16)
            return carry

        lax.fori_loop(0, NX, bwd_one, 0)
        for g in range(NB):
            out = jnp.dot(bk[g], blocks[g], preferred_element_type=F32).astype(BF16)
            for q in range(NX):
                gf_ref[span(q * quarter + t * TILE, TILE), g * BLK : (g + 1) * BLK] = out[
                    q * TILE : (q + 1) * TILE
                ]
        for q in range(NX):
            part = span(q * quarter + t * TILE, TILE)
            copy = pltpu.make_async_copy(gf_ref.at[part], gf_hbm.at[part], out_sem.at[t, q])
            copy.start()
            written.append(copy)

    pltpu.make_async_copy(act, act, a2a_recv[1].at[0]).wait()

    def weight(h, carry):
        g = lax.dot_general(
            cot[h], act[...], (((1,), (1,)), ((), ())), preferred_element_type=F32
        ).astype(BF16)
        for i in range(4):
            gst[i % 2, h // 2, (h % 2) * 2 + i // 2] = g[i * group : (i + 1) * group]
        return carry

    for i in range(NX):
        lax.fori_loop(2 * i, 2 * i + 2, weight, 0)
        pltpu.make_async_remote_copy(
            src_ref=gst.at[1 - c, i], dst_ref=rc.at[i],
            send_sem=g_send.at[0], recv_sem=g_recv.at[0],
            device_id={"rows": row + 1 - 2 * c}, device_id_type=MESH,
        ).start()

    cross_bwd(0)

    pltpu.make_async_copy(rc, rc, g_recv.at[0]).wait()
    for i in range(NX):
        p1[i] = (gst[c, i].astype(F32) + rc[i].astype(F32)).astype(BF16)

    def gx(i, carry):
        other = (x + i) % NX
        pltpu.make_async_remote_copy(
            src_ref=p1.at[other], dst_ref=rx.at[x], send_sem=g_send.at[1], recv_sem=g_recv.at[1],
            device_id={"rows": other * NB + zc}, device_id_type=MESH,
        ).start()
        return carry

    lax.fori_loop(1, NX, gx, 0)
    pltpu.make_async_copy(p1.at[x], rx.at[x], g_recv.at[1]).start()

    cross_bwd(1)

    cross_bwd(2)

    pltpu.make_async_copy(rx, rx, g_recv.at[1]).wait()
    for i in range(NZ):
        total = rx[0, i].astype(F32)
        for j in range(1, NX):
            total = total + rx[j, i].astype(F32)
        p2[i] = total.astype(BF16)

    def gz(i, carry):
        other = (zl + i) % NZ
        pltpu.make_async_remote_copy(
            src_ref=p2.at[other], dst_ref=rz.at[zl], send_sem=g_send.at[2], recv_sem=g_recv.at[2],
            device_id={"rows": x * NB + other * NC + c}, device_id_type=MESH,
        ).start()
        return carry

    lax.fori_loop(1, NZ, gz, 0)
    pltpu.make_async_copy(p2.at[zl], rz.at[zl], g_recv.at[2]).start()

    for t in range(tiles):
        local_bwd(t)

    pltpu.make_async_copy(rz, rz, g_recv.at[2]).wait()
    total = rz[0].astype(F32)
    for j in range(1, NZ):
        total = total + rz[j].astype(F32)
    gw_ref[...] = total * (1.0 / (tok * ROWS) ** 0.5)
    copy = pltpu.make_async_copy(gw_ref, gw_hbm, loc_sem.at[5])
    copy.start()
    written.append(copy)
    for copy in written:
        copy.wait()

    for step, src in enumerate((s1, s2, s3, s4)):
        for part in (src.at[0:3], src.at[3, 0:7]):
            pltpu.make_async_copy(part, part, a2a_send[step].at[0]).wait()
    pltpu.make_async_copy(twst.at[0:7], twst.at[0:7], tw_send.at[0]).wait()
    pltpu.make_async_copy(twall.at[0:3], twall.at[0:3], tw_send.at[1]).wait()
    for copy in sent:
        copy.wait_send()
    pltpu.make_async_copy(rc, rc, g_send.at[0]).wait()
    pltpu.make_async_copy(p1.at[0:3], p1.at[0:3], g_send.at[1]).wait()
    pltpu.make_async_copy(p2.at[0:3], p2.at[0:3], g_send.at[2]).wait()


def hand_over(gf_in, gw_in, gf_out, gw_out):
    gf_out[...] = gf_in[...]
    gw_out[...] = gw_in[...]


def per_device(features, cotangent, blocks, twiddles, channel_weight):
    chan, tok = features.shape
    quarter = chan // NX
    group = channel_weight.shape[1] // ROWS
    piece = (NX, NB, quarter, BLK)
    vm = pltpu.VMEM
    dma = pltpu.SemaphoreType.DMA
    scratch = [
        vm((chan, tok), BF16), vm(blocks.shape, BF16), vm(twiddles.shape, F32),
        vm(channel_weight.shape, BF16), vm((CHS, chan, tok), BF16),
        vm((NB, 2 * LEVELS, BLK), BF16), vm((NB, 2 * LEVELS, BLK), BF16),
        vm((NX, NB, 2 * LEVELS, BLK), BF16),
        vm((2, CROSS, ROWS, 8, BLK), F32), vm((2, LOCAL, NB, 8, BLK), F32),
        vm((NB, NX * TILE, BLK), F32), vm((chan, tok), BF16), vm(piece, F32),
        *[vm(piece, BF16)] * 7, vm((NB, NX * TILE, BLK), BF16),
        vm((NC, NX, NZ, group, chan), BF16), vm((NX, NZ, group, chan), BF16),
        vm((NX, NZ, group, chan), BF16), vm((NX, NZ, group, chan), BF16),
        vm((NZ, group, chan), BF16), vm((NZ, group, chan), BF16),
        vm((chan, tok), BF16), vm((group, chan), F32), dma((3, NX)),
        dma((6,)), *[dma((1,))] * 4, *[dma((3,))] * 4, dma((2,)), dma((2,)),
        dma((CHUNKS,)), dma((CHUNKS,)), dma((4, CHUNKS, 2)), dma((4, CHUNKS, 2)),
        dma((3,)), dma((3,)),
    ]
    grad_features, grad_weight = pl.pallas_call(
        body,
        out_shape=(
            jax.ShapeDtypeStruct((chan, tok), BF16),
            jax.ShapeDtypeStruct((group, chan), F32),
        ),
        in_specs=[pl.BlockSpec(memory_space=pltpu.HBM)] * 5,
        out_specs=(pl.BlockSpec(memory_space=pl.ANY),) * 2,
        scratch_shapes=scratch,
        name="mixer",
        compiler_params=pltpu.CompilerParams(
            collective_id=0, has_side_effects=True, vmem_limit_bytes=60 << 20
        ),
    )(features, cotangent, blocks, twiddles, channel_weight)
    steps = [
        pl.BlockSpec((chan // PARTS, tok), lambda i: (i, 0)),
        pl.BlockSpec((group, chan), lambda i: (0, 0)),
    ]
    grad_features, grad_weight = pl.pallas_call(
        hand_over,
        out_shape=(
            jax.ShapeDtypeStruct((chan, tok), BF16),
            jax.ShapeDtypeStruct((group, chan), F32),
        ),
        grid=(PARTS,),
        in_specs=steps,
        out_specs=steps,
        name="hand_over",
        compiler_params=pltpu.CompilerParams(vmem_limit_bytes=60 << 20),
    )(grad_features, grad_weight)
    return grad_features, grad_weight.T


def solution(mesh):
    return jax.shard_map(
        per_device,
        mesh=mesh,
        in_specs=(
            P("ch", "rows"),
            P("ch", "rows"),
            P("rows", None, None),
            P(None, None, "rows"),
            P("ch", None),
        ),
        out_specs=(P("ch", "rows"), P("ch", "rows")),
        check_vma=False,
    )
```
